32 devices in a mesh: segment: 4 (over x, core), fsdp: 2 (over y), dp: 4 (over z).
Axes of the slice: x: 2, y: 2, z: 4, core: 2. Of those that a mesh axis runs over, the one named last changes fastest.
Arguments:
- inputs: bfloat16 [3, 16, 49, 2880], P(None, ('fsdp', 'dp')), may hold values from -6 to 6
- cotangent: bfloat16 [3, 16, 49, 2880], P(None, ('fsdp', 'dp')), may hold values from -0.119628906 to 0.119628906
- plan: int32 [3], replicated, may hold values from 0 to 2, each once
- weight: bfloat16 [4, 2880, 2880], P('segment', 'fsdp'), may hold values from -0.109375 to 0.109375
- squeeze: bfloat16 [4, 2880, 360], P('segment', 'fsdp'), may hold values from -0.109375 to 0.109375
- excite: bfloat16 [4, 2880, 360], P('segment', 'fsdp'), may hold values from -0.3125 to 0.3125
Outputs:
- grad_weight: float32 [4, 2880, 2880], P('segment', ('fsdp', 'dp'))
- grad_squeeze: float32 [4, 2880, 360], P('segment', ('fsdp', 'dp'))
- grad_excite: float32 [4, 2880, 360], P('segment', ('fsdp', 'dp'))
The draws below stay inside these ranges and needn't reach their ends.
Inputs may be any that keep to these rules, and one draw needn't show every extreme that they name: plan names each of the 3 microbatches exactly once.
All inputs are finite; a program needn't handle non-finite values.
Results may differ from the reference program's by a relative error of at most 0.024.
Values may be sent and summed in bfloat16 or wider, within the bound.
No kernel may reach another device: no remote copies, remote signals or barrier semaphores. Data moves between devices by JAX's collectives and lax.ppermute only.
A program may use at most 128 MiB of HBM per device.

```python
import jax
import jax.numpy as jnp
from jax import lax

C = 2880
R = 360
PIX = 49
MICRO = 3
IMG_DEV = 2
IMAGES = 16
SEGMENTS = 4
N_SEGMENT = 4


def block_levels(stream_key, dims, shards, least, top_value):
    def one(position, blocks):
        steps = jax.random.uniform(jax.random.fold_in(jax.random.fold_in(stream_key, 6), position), (blocks,), jnp.float32, least / len(shards), top_value / len(shards))
        return jnp.repeat(jnp.exp(steps), dims[position] // blocks).reshape((-1,) + (1,) * (len(dims) - position - 1))

    gain = one(*shards[0])
    for cut in shards[1:]:
        gain = gain * one(*cut)
    return gain


def noise(key, extent, scale, reach, cuts=(), held_as=jnp.bfloat16):
    factor_of = block_levels(key, extent, cuts, -0.22, 0.18) if cuts else 1.0
    array = jax.random.normal(key, extent, jnp.float32) * scale * factor_of
    return jnp.minimum(jnp.maximum(array, -reach), reach).astype(held_as)


def setup_inputs(seed: int = 0) -> dict:
    splits = jax.random.split(jax.random.key(seed), 7)
    return {
        "inputs": noise(splits[0], (MICRO, IMAGES, PIX, C), 1.0, 6.0, ((1, 8),)),
        "cotangent": noise(splits[1], (MICRO, IMAGES, PIX, C), 0.02, 0.119628906, ((1, 8),)),
        "plan": jax.random.permutation(splits[2], MICRO).astype(jnp.int32),
        "weight": noise(splits[3], (SEGMENTS, C, C), C ** -0.5, 0.109375, ((0, 4), (1, 2))),
        "squeeze": noise(splits[4], (SEGMENTS, C, R), C ** -0.5, 0.109375, ((0, 4), (1, 2))),
        "excite": noise(splits[5], (SEGMENTS, C, R), R ** -0.5, 0.3125, ((0, 4), (1, 2))),
    }


def silu_slope(value):
    sigma = jax.nn.sigmoid(value)
    return sigma * (1.0 + value * (1.0 - sigma))


def contract_rows(left, right):
    return lax.dot_general(left, right, (((0,), (0,)), ((), ())), preferred_element_type=jnp.float32)


def contract_cols(left, right):
    return lax.dot_general(left, right, (((1,), (1,)), ((), ())), preferred_element_type=jnp.float32)


def project(images, matrix):
    flat = images.reshape(-1, images.shape[-1])
    result = jnp.dot(flat, matrix, preferred_element_type=jnp.float32)
    return result.reshape(images.shape[:-1] + (matrix.shape[1],))


def forward_block(images, matrix, squeeze_w, excite_w):
    pre = project(images, matrix)
    active_map = jax.nn.silu(pre).astype(jnp.bfloat16)
    pooled = jnp.mean(active_map.astype(jnp.float32), axis=1).astype(jnp.bfloat16)
    squeezed = jnp.dot(pooled, squeeze_w, preferred_element_type=jnp.float32)
    hidden = jax.nn.silu(squeezed).astype(jnp.bfloat16)
    gate = jax.nn.sigmoid(contract_cols(hidden, excite_w))
    output = (images.astype(jnp.float32) + active_map.astype(jnp.float32) * gate[:, None, :]).astype(jnp.bfloat16)
    return output, pre, pooled, squeezed, hidden, gate


def backward_block(images, pre, squeezed, gate, upstream, matrix, squeeze_w, excite_w):
    active_map = jax.nn.silu(pre).astype(jnp.bfloat16)
    upper = upstream.astype(jnp.float32)
    d_act = upper * gate[:, None, :]
    d_gate = jnp.sum(upper * active_map.astype(jnp.float32), axis=1)
    d_excite = (d_gate * gate * (1.0 - gate)).astype(jnp.bfloat16)
    d_hidden = jnp.dot(d_excite, excite_w, preferred_element_type=jnp.float32)
    d_squeezed = (d_hidden * silu_slope(squeezed)).astype(jnp.bfloat16)
    d_pooled = contract_cols(d_squeezed, squeeze_w)
    d_act = d_act + d_pooled[:, None, :] / images.shape[1]
    d_pre = (d_act * silu_slope(pre)).astype(jnp.bfloat16)
    flat = d_pre.reshape(-1, d_pre.shape[-1])
    back = contract_cols(flat, matrix).reshape(images.shape)
    d_images = (upper + back).astype(jnp.bfloat16)
    return d_excite, d_squeezed, d_pre, d_images


def group_sum(left, right, micro, groups):
    width_l = left.shape[-1]
    width_r = right.shape[-1]
    left_g = left.reshape(micro, groups, -1, width_l).transpose(1, 0, 2, 3).reshape(groups, -1, width_l)
    right_g = right.reshape(micro, groups, -1, width_r).transpose(1, 0, 2, 3).reshape(groups, -1, width_r)

    def add_group(total, pair):
        term = contract_rows(pair[0], pair[1])
        term = lax.optimization_barrier(term.astype(jnp.bfloat16)).astype(jnp.float32)
        return total + term, None

    total, unused = lax.scan(add_group, jnp.zeros((width_l, width_r), jnp.float32), (left_g, right_g))
    return total


def reference(inputs, cotangent, plan, weight, squeeze, excite):
    ordered = inputs[plan]
    micro, images, pixels, width = ordered.shape
    groups = images // IMG_DEV
    current = ordered.reshape(micro * images, pixels, width)
    saved = []
    for segment in range(N_SEGMENT):
        output, pre, pooled, squeezed, hidden, gate = forward_block(current, weight[segment], squeeze[segment], excite[segment])
        saved.append((current, pre, pooled, squeezed, hidden, gate))
        current = output
    upstream = cotangent.reshape(micro * images, pixels, width)
    grads_w = []
    grads_s = []
    grads_e = []
    for segment in reversed(range(N_SEGMENT)):
        images_in, pre, pooled, squeezed, hidden, gate = saved[segment]
        d_excite, d_squeezed, d_pre, d_images = backward_block(images_in, pre, squeezed, gate, upstream, weight[segment], squeeze[segment], excite[segment])
        grads_w.append(group_sum(images_in, d_pre, micro, groups))
        grads_s.append(group_sum(pooled, d_squeezed, micro, groups))
        grads_e.append(group_sum(d_excite, hidden, micro, groups))
        upstream = d_images
    grads_w = grads_w[::-1]
    grads_s = grads_s[::-1]
    grads_e = grads_e[::-1]
    return (jnp.stack(grads_w), jnp.stack(grads_s), jnp.stack(grads_e))
```

```python
import functools

import jax
import jax.numpy as jnp
from jax import lax
from jax.experimental import pallas as pl
from jax.experimental.pallas import tpu as pltpu
from jax.sharding import PartitionSpec as P

BF = jnp.bfloat16
F32 = jnp.float32
SUB = 8
PIECES = 3
VMEM_LIMIT = 62 * 1024 * 1024


def up(value, step):
    return -(-value // step) * step


def silu_slope(value):
    sigma = jax.nn.sigmoid(value)
    return sigma * (1.0 + value * (1.0 - sigma))


def nn(left, right):
    return lax.dot_general(left, right, (((1,), (0,)), ((), ())), preferred_element_type=F32)


def nt(left, right):
    return lax.dot_general(left, right, (((1,), (1,)), ((), ())), preferred_element_type=F32)


def tn(left, right):
    return lax.dot_general(left, right, (((0,), (0,)), ((), ())), preferred_element_type=F32)


class Loader:
    def __init__(self, meta, own, other, bufs, sems):
        self.meta, self.own, self.other, self.bufs, self.sems = meta, own, other, bufs, sems

    def copies(self, block, refs):
        w_pieces, s_pieces = refs
        w_buf, s_buf, e_buf = self.bufs
        slot = 0
        for index, piece in enumerate(w_pieces):
            rows = piece.shape[0]
            at = pl.ds(pl.multiple_of(self.meta[1 + index], 16), rows)
            yield pltpu.make_async_copy(piece, w_buf.at[block, at], self.sems.at[block, slot])
            slot += 1
        for index, piece in enumerate(s_pieces):
            rows = piece.shape[0] // 2
            at = pl.ds(pl.multiple_of(self.meta[1 + len(w_pieces) + index], 16), rows)
            for half, buf in enumerate((s_buf, e_buf)):
                source = piece.at[pl.ds(half * rows, rows)]
                yield pltpu.make_async_copy(source, buf.at[block, at], self.sems.at[block, slot])
                slot += 1

    def start(self, block):
        @pl.when(self.meta[0] == block)
        def _():
            for copy in self.copies(block, self.own):
                copy.start()

        @pl.when(self.meta[0] != block)
        def _():
            for copy in self.copies(block, self.other):
                copy.start()

    def wait(self, block):
        for copy in self.copies(block, self.own):
            copy.wait()


def image_masks(rows, images, pixels):
    row = lax.broadcasted_iota(jnp.int32, (rows, 1), 0)
    return [(row >= i * pixels) & (row < (i + 1) * pixels) for i in range(images)]


def per_image(value, masks):
    slot = lax.broadcasted_iota(jnp.int32, (SUB, 1), 0)
    total = jnp.zeros((SUB, value.shape[1]), F32)
    for i, mask in enumerate(masks):
        summed = jnp.sum(jnp.where(mask, value, 0.0), axis=0, keepdims=True)
        total = jnp.where(slot == i, summed, total)
    return total


def per_row(value, masks):
    spread = jnp.zeros((masks[0].shape[0], value.shape[1]), F32)
    for i, mask in enumerate(masks):
        spread = jnp.where(mask, value[i : i + 1, :], spread)
    return spread


def forward_kernel(cfg, meta, h_ref, *refs):
    n_w, n_s, images, pixels, tiles = cfg
    pieces, refs = refs[: 2 * (n_w + n_s)], refs[2 * (n_w + n_s) :]
    own = (pieces[:n_w], pieces[n_w : n_w + n_s])
    other = (pieces[n_w + n_s : 2 * n_w + n_s], pieces[2 * n_w + n_s :])
    mid_ref, out_ref, pre_ref, gate_ref, sq_ref, pool_ref, hid_ref = refs[:7]
    w_buf, s_buf, e_buf, act_ref, sems = refs[7:]
    loader = Loader(meta, own, other, (w_buf, s_buf, e_buf), sems)
    loader.start(0)
    loader.start(1)
    masks = image_masks(h_ref.shape[0], images, pixels)
    for block, (src, dst) in enumerate(((h_ref, mid_ref), (mid_ref, out_ref))):
        loader.wait(block)
        squeezed = jnp.zeros(sq_ref.shape[1:], F32)
        for low, width in tiles:
            cols = slice(low, low + width)
            pre = nn(src[...], w_buf[block, :, cols])
            pre_ref[block, :, cols] = pre
            active = (pre * jax.nn.sigmoid(pre)).astype(BF)
            act_ref[:, cols] = active
            pooled = (per_image(active.astype(F32), masks) / pixels).astype(BF)
            pool_ref[block, :, cols] = pooled.astype(F32)
            squeezed = squeezed + nn(pooled, s_buf[block, cols, :])
        sq_ref[block] = squeezed
        hidden = (squeezed * jax.nn.sigmoid(squeezed)).astype(BF)
        hid_ref[block] = hidden.astype(F32)
        for low, width in tiles:
            cols = slice(low, low + width)
            gate = jax.nn.sigmoid(nt(hidden, e_buf[block, cols, :]))
            gate_ref[block, :, cols] = gate
            gated = act_ref[:, cols].astype(F32) * per_row(gate, masks)
            dst[:, cols] = (src[:, cols].astype(F32) + gated).astype(BF)


def backward_kernel(cfg, meta, up_ref, pre_ref, gate_ref, sq_ref, *refs):
    n_w, n_s, images, pixels, tiles = cfg
    pieces, refs = refs[: 2 * (n_w + n_s)], refs[2 * (n_w + n_s) :]
    own = (pieces[:n_w], pieces[n_w : n_w + n_s])
    other = (pieces[n_w + n_s : 2 * n_w + n_s], pieces[2 * n_w + n_s :])
    out_ref, dpre_ref, dsq_ref, dex_ref = refs[:4]
    w_buf, s_buf, e_buf, mid_ref, flat_ref, sems = refs[4:]
    loader = Loader(meta, own, other, (w_buf, s_buf, e_buf), sems)
    loader.start(1)
    loader.start(0)
    masks = image_masks(up_ref.shape[0], images, pixels)
    for block, src, dst in ((1, up_ref, mid_ref), (0, mid_ref, out_ref)):
        loader.wait(block)
        d_hidden = jnp.zeros(dsq_ref.shape[1:], F32)
        for low, width in tiles:
            cols = slice(low, low + width)
            pre = pre_ref[block, :, cols]
            active = (pre * jax.nn.sigmoid(pre)).astype(BF).astype(F32)
            d_gate = per_image(src[:, cols].astype(F32) * active, masks)
            gate = gate_ref[block, :, cols]
            d_excite = (d_gate * gate * (1.0 - gate)).astype(BF)
            dex_ref[block, :, cols] = d_excite.astype(F32)
            d_hidden = d_hidden + nn(d_excite, e_buf[block, cols, :])
        d_squeezed = (d_hidden * silu_slope(sq_ref[block])).astype(BF)
        dsq_ref[block] = d_squeezed.astype(F32)
        for tile, (low, width) in enumerate(tiles):
            cols = slice(low, low + width)
            pre = pre_ref[block, :, cols]
            d_pool = nt(d_squeezed, s_buf[block, cols, :]) / pixels
            d_act = src[:, cols].astype(F32) * per_row(gate_ref[block, :, cols], masks)
            d_act = d_act + per_row(d_pool, masks)
            d_pre = (d_act * silu_slope(pre)).astype(BF)
            flat_ref[:, cols] = d_pre
            if width < dpre_ref.shape[3]:
                dpre_ref[block, tile] = jnp.zeros(dpre_ref.shape[2:], BF)
            dpre_ref[block, tile, :, :width] = d_pre
        for low, width in tiles:
            cols = slice(low, low + width)
            back = nt(flat_ref[...], w_buf[block, cols, :])
            dst[:, cols] = (src[:, cols].astype(F32) + back).astype(BF)


def run_pass(kernel, cfg, meta, dense, sets, outs, scratch, channels, hidden, flops):
    own, other = sets
    pieces = [*own[0], *own[1], *other[0], *other[1]]
    copies = len(own[0]) + 2 * len(own[1])
    vmem = pl.BlockSpec(memory_space=pltpu.VMEM)
    return pl.pallas_call(
        functools.partial(kernel, cfg),
        out_shape=[jax.ShapeDtypeStruct(shape, dtype) for shape, dtype in outs],
        in_specs=[pl.BlockSpec(memory_space=pltpu.SMEM)]
        + [vmem] * len(dense)
        + [pl.BlockSpec(memory_space=pl.ANY)] * len(pieces),
        out_specs=[vmem] * len(outs),
        scratch_shapes=[
            pltpu.VMEM((2, channels, channels), BF),
            pltpu.VMEM((2, channels, hidden), BF),
            pltpu.VMEM((2, channels, hidden), BF),
            *scratch,
            pltpu.SemaphoreType.DMA((2, copies)),
        ],
        compiler_params=pltpu.CompilerParams(vmem_limit_bytes=VMEM_LIMIT),
        cost_estimate=pl.CostEstimate(
            flops=flops, bytes_accessed=2 * 2 * channels * (channels + 2 * hidden), transcendentals=0
        ),
    )(meta, *dense, *pieces)


def swap(value, axis, stride=1):
    count = lax.axis_size(axis)
    return lax.ppermute(value, axis, [(i, i ^ stride) for i in range(count)])


def rotate(value, axis, steps):
    count = lax.axis_size(axis)
    return lax.ppermute(value, axis, [(i, (i + steps) % count) for i in range(count)])


def over_fsdp(value):
    count = lax.axis_size("fsdp")
    return [value] + [rotate(value, "fsdp", -step) for step in range(1, count)]


def gather_weights(weight, squeeze, excite):
    fsdp, dp = lax.axis_size("fsdp"), lax.axis_size("dp")
    rows = weight.shape[0]
    pair = jnp.concatenate([squeeze, excite], axis=0)
    if fsdp != 2 or dp % 2 or rows % (2 * 16 * PIECES):
        whole = lax.all_gather(weight, "fsdp", axis=0, tiled=True)
        both = [lax.all_gather(part, "fsdp", axis=0, tiled=True) for part in (squeeze, excite)]
        zero = jnp.int32(0)
        return [whole], [jnp.concatenate(both, axis=0)], [zero], [zero]
    mine = lax.axis_index("fsdp") * rows
    far = rows - mine
    parity = lax.axis_index("dp") % 2
    half = rows // 2
    step = half // PIECES
    near_at = far + parity * half
    cross_at = far + (1 - parity) * half
    near_s = swap(
        jnp.concatenate(
            [lax.dynamic_slice_in_dim(part, parity * half, half, 0) for part in (squeeze, excite)], 0
        ),
        "fsdp",
    )
    near = [
        swap(lax.dynamic_slice_in_dim(weight, parity * half + i * step, step, 0), "fsdp")
        for i in range(PIECES)
    ]
    cross_s = swap(near_s, "dp")
    cross = [swap(part, "dp") for part in near]
    w_at = [mine] + [near_at + i * step for i in range(PIECES)]
    w_at += [cross_at + i * step for i in range(PIECES)]
    return [weight, *near, *cross], [pair, near_s, cross_s], w_at, [mine, near_at, cross_at]


def shifted(value, axis, steps):
    count = lax.axis_size(axis)
    leading, last = (max(0, -steps), min(count, count - steps))
    return lax.ppermute(value, axis, [(source, source + steps) for source in range(leading, last)])


def on_device(inputs, cotangent, plan, weight, squeeze, excite):
    fsdp, dp = lax.axis_size("fsdp"), lax.axis_size("dp")
    sections = lax.axis_size("segment")
    section = lax.axis_index("segment")
    core = section % 2
    mesh_f, mesh_z = lax.axis_index("fsdp"), lax.axis_index("dp")
    micro, images_dev, pixels, channels = inputs.shape
    hidden = squeeze.shape[2]
    per_core = images_dev // 2
    images = micro * per_core
    rows = up(images * pixels, 16)
    group = up(-(-channels // dp), 128)
    tiles = [(low, min(group, channels - low)) for low in range(0, channels, group)]

    w_own, s_own, w_at, s_at = gather_weights(weight[0], squeeze[0], excite[0])
    w_other = [swap(part, "segment") for part in w_own]
    s_other = [swap(part, "segment") for part in s_own]
    sets = ((w_own, s_own), (w_other, s_other))
    meta = jnp.stack([core, *w_at, *s_at]).astype(jnp.int32)
    cfg = (len(w_own), len(s_own), images, pixels, tiles)

    def flat(maps):
        mine = lax.dynamic_slice_in_dim(maps, core * per_core, per_core, 1)
        mine = mine.reshape(images * pixels, channels)
        return jnp.pad(mine, ((0, rows - images * pixels), (0, 0)))

    def forward_pass(h_in):
        outs = [
            ((rows, channels), BF),
            ((rows, channels), BF),
            ((2, rows, channels), F32),
            ((2, SUB, channels), F32),
            ((2, SUB, hidden), F32),
            ((2, SUB, channels), F32),
            ((2, SUB, hidden), F32),
        ]
        scratch = [pltpu.VMEM((rows, channels), BF)]
        flops = 4 * rows * channels * channels
        return run_pass(
            forward_kernel, cfg, meta, [h_in], sets, outs, scratch, channels, hidden, flops
        )

    def backward_pass(d_out, pre, gate, sq):
        outs = [
            ((rows, channels), BF),
            ((2, len(tiles), rows, group), BF),
            ((2, SUB, hidden), F32),
            ((2, SUB, channels), F32),
        ]
        scratch = [pltpu.VMEM((rows, channels), BF), pltpu.VMEM((rows, channels), BF)]
        flops = 4 * rows * channels * channels
        return run_pass(
            backward_kernel,
            cfg,
            meta,
            [d_out, pre, gate, sq],
            sets,
            outs,
            scratch,
            channels,
            hidden,
            flops,
        )

    stages = sections // 2
    stage = section // 2
    h_in = flat(inputs[plan])
    d_in = flat(cotangent)
    kept = None
    for step in range(stages):
        mid, out, pre, gate, sq, pool, hid = forward_pass(h_in)
        new = (h_in, mid, pre, gate, sq, pool, hid)
        last = new
        if step == 0:
            kept = new
        elif step < stages - 1:
            kept = [jnp.where(stage == step, a, b) for a, b in zip(new, kept)]
        if step < stages - 1:
            h_in = shifted(out, "segment", 2)
    final = stage == stages - 1
    h_a, h_b, pool, hid = [
        jnp.where(final, last[i], kept[i]) for i in (0, 1, 5, 6)
    ]

    def swap_blocks(first, second):
        keep = jnp.where(core == 0, first, second)
        give = jnp.where(core == 0, second, first)
        return keep, swap(give, "segment")

    part = channels // fsdp

    def channel_part(value, owner):
        return lax.dynamic_slice_in_dim(value, owner * part, part, 1)

    h_pair = jnp.concatenate(swap_blocks(h_a, h_b), axis=0)
    h_mine = [channel_part(h_pair, mesh_f)]
    for step in range(1, fsdp):
        h_mine.append(rotate(channel_part(h_pair, (mesh_f - step) % fsdp), "fsdp", -step))
    h_mine = jnp.concatenate(h_mine, axis=0)
    h_all = lax.all_gather(h_mine, "dp", axis=0, tiled=False)
    early = jnp.concatenate([pool, hid], axis=2).astype(BF)
    early = jnp.concatenate(swap_blocks(early[0], early[1]), axis=0)
    early = lax.all_gather(early, ("fsdp", "dp"), axis=0, tiled=True)

    result = backward_pass(d_in, *last[2:5])
    for step in range(1, stages):
        d_out = shifted(result[0], "segment", -2)
        saved = kept[2:5]
        new = backward_pass(d_out, *saved)
        here = stage == stages - 1 - step
        result = [new[0]] + [jnp.where(here, a, b) for a, b in zip(new[1:], result[1:])]
    d_pre, d_sq, d_ex = result[1:]

    late = jnp.concatenate([d_ex, d_sq], axis=2).astype(BF)
    late = jnp.concatenate(swap_blocks(late[0], late[1]), axis=0)
    late = lax.all_gather(late, ("fsdp", "dp"), axis=0, tiled=True)

    d_pair = jnp.concatenate(swap_blocks(d_pre[0], d_pre[1]), axis=1)
    total = None
    for step in range(dp):
        piece = lax.dynamic_index_in_dim(d_pair, (mesh_z + step) % dp, 0, keepdims=False)
        if step:
            piece = rotate(piece, "dp", step)
        piece = jnp.concatenate(over_fsdp(piece), axis=0)
        source = lax.dynamic_index_in_dim(h_all, (mesh_z - step) % dp, 0, keepdims=False)
        term = tn(source, piece)
        total = term if total is None else total + term
    total = total.astype(BF)
    own_rows = part // dp
    gathered = jnp.zeros((dp, own_rows, group), BF)
    for step in range(dp):
        block = lax.dynamic_slice_in_dim(total, ((mesh_z + step) % dp) * own_rows, own_rows, 0)
        if step:
            block = rotate(block, "dp", step)
        gathered = lax.dynamic_update_index_in_dim(gathered, block, (mesh_z - step) % dp, 0)
    grad_w = jnp.concatenate([gathered[i, :, :w] for i, (_, w) in enumerate(tiles)], axis=1)

    first = mesh_f * part + mesh_z * own_rows
    pool_rows = lax.dynamic_slice_in_dim(early[:, :channels], first, own_rows, 1)
    dex_rows = lax.dynamic_slice_in_dim(late[:, :channels], first, own_rows, 1)
    grad_s = tn(pool_rows, late[:, channels:])
    grad_e = tn(dex_rows, early[:, channels:])
    return (grad_w.astype(F32)[None], grad_s[None], grad_e[None])


def solution(mesh):
    placed = (
        P(None, ("fsdp", "dp"), None, None),
        P(None, ("fsdp", "dp"), None, None),
        P(),
        P("segment", "fsdp", None),
        P("segment", "fsdp", None),
        P("segment", "fsdp", None),
    )
    return jax.shard_map(
        on_device,
        mesh=mesh,
        in_specs=placed,
        out_specs=(
            P("segment", ("fsdp", "dp"), None),
            P("segment", ("fsdp", "dp"), None),
            P("segment", ("fsdp", "dp"), None),
        ),
        check_vma=False,
    )
```

```python
import functools
import itertools

import jax
import jax.numpy as jnp
from jax import lax
from jax.experimental import pallas as pl
from jax.experimental.pallas import tpu as pltpu
from jax.sharding import PartitionSpec as P

BF = jnp.bfloat16
F32 = jnp.float32
SUB = 8
PIECES = 3
VMEM_LIMIT = 62 * 1024 * 1024


def up(value, step):
    return -(-value // step) * step


def silu_slope(value):
    sigma = jax.nn.sigmoid(value)
    return sigma * (1.0 + value * (1.0 - sigma))


def nn(left, right):
    return lax.dot_general(left, right, (((1,), (0,)), ((), ())), preferred_element_type=F32)


def nt(left, right):
    return lax.dot_general(left, right, (((1,), (1,)), ((), ())), preferred_element_type=F32)


def tn(left, right):
    return lax.dot_general(left, right, (((0,), (0,)), ((), ())), preferred_element_type=F32)


class Loader:
    def __init__(self, meta, own, other, n_w, tiles):
        self.core, self.at, self.own, self.other = meta[0], meta, own, other
        self.n_w, self.tiles = n_w, tiles

    def place(self, index, rows):
        return pl.ds(pl.multiple_of(self.at[3 + index], 16), rows)

    def weight(self, refs, buf, sems, tile):
        low, width = self.tiles[tile]
        cols = pl.ds(low, width)
        for index, piece in enumerate(refs[: self.n_w]):
            target = buf.at[self.place(index, piece.shape[0]), cols]
            yield pltpu.make_async_copy(piece.at[:, cols], target, sems.at[tile, index])

    def pair(self, refs, bufs, sems):
        for index, piece in enumerate(refs[self.n_w :]):
            rows = piece.shape[0] // 2
            at = self.place(self.n_w + index, rows)
            for half, buf in enumerate(bufs):
                source = piece.at[pl.ds(half * rows, rows)]
                yield pltpu.make_async_copy(source, buf.at[at], sems.at[half, index])

    def start(self, block, kind, *args):
        for mine, refs in ((True, self.own), (False, self.other)):

            @pl.when((self.core == block) == mine)
            def _():
                for copy in kind(refs, *args):
                    copy.start()

    def wait(self, kind, *args):
        for copy in kind(self.own, *args):
            copy.wait()


def halves(value_ref, mine_ref, give_ref, index):
    part = mine_ref.shape[1]
    for here in range(value_ref.shape[1] // part):

        @pl.when(index == here)
        def _():
            mine_ref[...] = value_ref[:, here * part : (here + 1) * part]
            there = 1 - here
            give_ref[...] = value_ref[:, there * part : (there + 1) * part]


def pick_kernel(cfg, meta, order, all_ref, *refs):
    images, pixels, images_dev = cfg
    out_ref = refs[0]
    rows, count = out_ref.shape[0], all_ref.shape[0]
    per_core = images_dev // 2
    row = lax.broadcasted_iota(jnp.int32, (rows, 1), 0)
    target = jnp.full((rows, 1), -1, jnp.int32)
    for i in range(images):
        micro, slot = divmod(i, per_core)
        first = order[micro] * (pixels * images_dev) + meta[0] * per_core + slot
        inside = (row >= i * pixels) & (row < (i + 1) * pixels)
        target = jnp.where(inside, first + (row - i * pixels) * images_dev, target)
    chosen = lax.broadcasted_iota(jnp.int32, (rows, count), 1) == target
    chosen = jnp.where(chosen, 1.0, 0.0).astype(BF)
    out_ref[...] = nn(chosen, all_ref[...]).astype(BF)
    if len(refs) > 1:
        halves(out_ref, refs[1], refs[2], meta[2])


def partial_kernel(cfg, block, meta, mine_ref, recv_ref, own, other, keep_ref, give_ref, *scratch):
    (tiles,) = cfg
    x_buf, w_buf, sems = scratch
    rows = mine_ref.shape[0]

    def copy(ref, tile):
        cols = pl.ds(*tiles[tile])
        return pltpu.make_async_copy(ref.at[:, cols], w_buf.at[:, cols], sems.at[tile])

    @pl.when(meta[1] == 1)
    def _():
        for here, ref in ((True, own), (False, other)):

            @pl.when((meta[0] == block) == here)
            def _():
                for tile in range(len(tiles)):
                    copy(ref, tile).start()

        x_buf[:rows] = mine_ref[...]
        x_buf[rows:] = recv_ref[...]
        for tile, (low, width) in enumerate(tiles):
            cols = slice(low, low + width)
            copy(own, tile).wait()
            both = nn(x_buf[...], w_buf[:, cols])
            keep_ref[:, cols] = both[:rows]
            give_ref[:, cols] = both[rows:].astype(BF)


def image_masks(rows, images, pixels):
    row = lax.broadcasted_iota(jnp.int32, (rows, 1), 0)
    return [(row >= i * pixels) & (row < (i + 1) * pixels) for i in range(images)]


def per_image(value, masks):
    slot = lax.broadcasted_iota(jnp.int32, (SUB, 1), 0)
    total = jnp.zeros((SUB, value.shape[1]), F32)
    for i, mask in enumerate(masks):
        summed = jnp.sum(jnp.where(mask, value, 0.0), axis=0, keepdims=True)
        total = jnp.where(slot == i, summed, total)
    return total


def per_row(value, masks):
    spread = jnp.zeros((masks[0].shape[0], value.shape[1]), F32)
    for i, mask in enumerate(masks):
        spread = jnp.where(mask, value[i : i + 1, :], spread)
    return spread


def gated_block(tiles, masks, pixels, pre_of, src, dst, s_buf, e_buf, act_ref, outs):
    pre_ref, gate_ref, sq_ref, pool_ref, hid_ref = outs
    squeezed = jnp.zeros(sq_ref.shape, F32)
    for tile, (low, width) in enumerate(tiles):
        cols = slice(low, low + width)
        pre = pre_of(tile, cols)
        pre_ref[:, cols] = pre
        active = (pre * jax.nn.sigmoid(pre)).astype(BF)
        act_ref[:, cols] = active
        pooled = (per_image(active.astype(F32), masks) / pixels).astype(BF)
        pool_ref[:, cols] = pooled.astype(F32)
        squeezed = squeezed + nn(pooled, s_buf[cols, :])
    sq_ref[...] = squeezed
    hidden = (squeezed * jax.nn.sigmoid(squeezed)).astype(BF)
    hid_ref[...] = hidden.astype(F32)
    for low, width in tiles:
        cols = slice(low, low + width)
        gate = jax.nn.sigmoid(nt(hidden, e_buf[cols, :]))
        gate_ref[:, cols] = gate
        gated = act_ref[:, cols].astype(F32) * per_row(gate, masks)
        dst[:, cols] = (src[:, cols].astype(F32) + gated).astype(BF)


def split_pieces(refs, n_w, n_s):
    count = n_w + n_s
    return refs[:count], refs[count : 2 * count], refs[2 * count :]


def gate_kernel(cfg, block, meta, h_ref, keep_ref, recv_ref, *refs):
    n_s, images, pixels, tiles, send = cfg
    own, other, refs = split_pieces(refs, 0, n_s)
    out_ref, outs, refs = refs[0], refs[1:6], refs[6:]
    sends, refs = refs[: 2 * send], refs[2 * send :]
    s_buf, e_buf, act_ref, sems = refs
    loader = Loader(meta, own, other, 0, tiles)

    @pl.when(meta[1] == 1)
    def _():
        loader.start(block, loader.pair, (s_buf, e_buf), sems)
        masks = image_masks(h_ref.shape[0], images, pixels)
        waited = []

        def pre_of(tile, cols):
            if not waited:
                waited.append(True)
                loader.wait(loader.pair, (s_buf, e_buf), sems)
            return keep_ref[:, cols] + recv_ref[:, cols].astype(F32)

        gated_block(
            tiles, masks, pixels, pre_of, h_ref, out_ref, s_buf, e_buf, act_ref, outs
        )
        if send:
            halves(out_ref, sends[0], sends[1], meta[2])


def forward_kernel(cfg, meta, h_ref, *refs):
    n_w, n_s, images, pixels, tiles = cfg
    own, other, refs = split_pieces(refs, n_w, n_s)
    mid_ref, out_ref = refs[:2]
    outs = (refs[2:7], refs[7:12])
    w_buf, s_buf, e_buf, act_ref, w_sems, s_sems = refs[12:]
    loader = Loader(meta, own, other, n_w, tiles)

    @pl.when(meta[1] == 1)
    def _():
        for block in range(2):
            loader.start(block, loader.weight, w_buf.at[block], w_sems.at[block], 0)
            pair = (s_buf.at[block], e_buf.at[block])
            loader.start(block, loader.pair, pair, s_sems.at[block])
            for tile in range(1, len(tiles)):
                loader.start(block, loader.weight, w_buf.at[block], w_sems.at[block], tile)
        masks = image_masks(h_ref.shape[0], images, pixels)
        for block, (src, dst) in enumerate(((h_ref, mid_ref), (mid_ref, out_ref))):

            def pre_of(tile, cols):
                loader.wait(loader.weight, w_buf.at[block], w_sems.at[block], tile)
                if tile == 0:
                    pair = (s_buf.at[block], e_buf.at[block])
                    loader.wait(loader.pair, pair, s_sems.at[block])
                return nn(src[...], w_buf[block, :, cols])

            gated_block(
                tiles,
                masks,
                pixels,
                pre_of,
                src,
                dst,
                s_buf.at[block],
                e_buf.at[block],
                act_ref,
                outs[block],
            )


def backward_kernel(cfg, meta, up_ref, *refs):
    n_w, n_s, images, pixels, tiles, through = cfg
    saved, refs = (refs[:3], refs[3:6]), refs[6:]
    own, other, refs = split_pieces(refs, n_w, n_s)
    outs, refs = (refs[:3], refs[3:6]), refs[6:]
    if through:
        end_ref, refs = refs[0], refs[1:]
    w_buf, s_buf, e_buf, mid_ref, flat_ref, w_sems, s_sems = refs
    loader = Loader(meta, own, other, n_w, tiles)
    weighted = (0, 1) if through else (1,)
    slot = {block: place for place, block in enumerate(weighted)}

    @pl.when(meta[1] == 1)
    def _():
        for block in (1, 0):
            pair = (s_buf.at[block], e_buf.at[block])
            loader.start(block, loader.pair, pair, s_sems.at[block])
        for block in reversed(weighted):
            for tile in range(len(tiles)):
                at = slot[block]
                loader.start(block, loader.weight, w_buf.at[at], w_sems.at[at], tile)
        masks = image_masks(up_ref.shape[0], images, pixels)
        for block, src in ((1, up_ref), (0, mid_ref)):
            pre_ref, gate_ref, sq_ref = saved[block]
            dpre_ref, dsq_ref, dex_ref = outs[block]
            pair = (s_buf.at[block], e_buf.at[block])
            loader.wait(loader.pair, pair, s_sems.at[block])
            d_hidden = jnp.zeros(dsq_ref.shape, F32)
            for low, width in tiles:
                cols = slice(low, low + width)
                pre = pre_ref[:, cols]
                active = (pre * jax.nn.sigmoid(pre)).astype(BF).astype(F32)
                d_gate = per_image(src[:, cols].astype(F32) * active, masks)
                gate = gate_ref[:, cols]
                d_excite = (d_gate * gate * (1.0 - gate)).astype(BF)
                dex_ref[:, cols] = d_excite.astype(F32)
                d_hidden = d_hidden + nn(d_excite, e_buf[block, cols, :])
            d_squeezed = (d_hidden * silu_slope(sq_ref[...])).astype(BF)
            dsq_ref[...] = d_squeezed.astype(F32)
            for tile, (low, width) in enumerate(tiles):
                cols = slice(low, low + width)
                pre = pre_ref[:, cols]
                d_pool = nt(d_squeezed, s_buf[block, cols, :]) / pixels
                d_act = src[:, cols].astype(F32) * per_row(gate_ref[:, cols], masks)
                d_act = d_act + per_row(d_pool, masks)
                d_pre = (d_act * silu_slope(pre)).astype(BF)
                flat_ref[:, cols] = d_pre
                if width < dpre_ref.shape[2]:
                    dpre_ref[tile] = jnp.zeros(dpre_ref.shape[1:], BF)
                dpre_ref[tile, :, :width] = d_pre
            if block not in slot:
                continue
            at = slot[block]
            for tile in range(len(tiles)):
                loader.wait(loader.weight, w_buf.at[at], w_sems.at[at], tile)
            dst = mid_ref if block else end_ref
            for low, width in tiles:
                cols = slice(low, low + width)
                back = nt(flat_ref[...], w_buf[at, cols, :])
                dst[:, cols] = (src[:, cols].astype(F32) + back).astype(BF)


def call(kernel, smem, dense, pieces, outs, scratch, flops, moved):
    vmem = pl.BlockSpec(memory_space=pltpu.VMEM)
    return pl.pallas_call(
        kernel,
        out_shape=[jax.ShapeDtypeStruct(shape, dtype) for shape, dtype in outs],
        in_specs=[pl.BlockSpec(memory_space=pltpu.SMEM)] * len(smem)
        + [vmem] * len(dense)
        + [pl.BlockSpec(memory_space=pl.ANY)] * len(pieces),
        out_specs=[vmem] * len(outs),
        scratch_shapes=scratch,
        compiler_params=pltpu.CompilerParams(vmem_limit_bytes=VMEM_LIMIT),
        cost_estimate=pl.CostEstimate(flops=flops, bytes_accessed=moved, transcendentals=0),
    )(*smem, *dense, *pieces)


def move(value, axes, target):
    sizes = [lax.axis_size(axis) for axis in axes]
    pairs = []
    for index in itertools.product(*[range(size) for size in sizes]):
        goal = target(*index)
        if goal is not None:
            flat = [0, 0]
            for size, a, b in zip(sizes, index, goal):
                flat = [flat[0] * size + a, flat[1] * size + b]
            pairs.append(tuple(flat))
    return lax.ppermute(value, axes, pairs)


def swap(value, axis, stride=1):
    count = lax.axis_size(axis)
    return lax.ppermute(value, axis, [(i, i ^ stride) for i in range(count)])


def rotate(value, axis, steps):
    count = lax.axis_size(axis)
    return lax.ppermute(value, axis, [(i, (i + steps) % count) for i in range(count)])


def over_fsdp(value):
    count = lax.axis_size("fsdp")
    return [value] + [rotate(value, "fsdp", -step) for step in range(1, count)]


def parity_half(value, parity, low, rows):
    return lax.dynamic_slice_in_dim(value, parity * (value.shape[0] // 2) + low, rows, 0)


def far_half(weight, parity, chosen):
    step = weight.shape[0] // 2 // PIECES
    cuts = [parity_half(weight, parity, i * step, step) for i in range(PIECES)]
    near = [
        move(cut, ("segment", "fsdp"), lambda s, f: (s, 1 - f) if s in chosen else None)
        for cut in cuts
    ]
    cross = [
        move(cut, ("segment", "dp"), lambda s, z: (s, z ^ 1) if s in chosen else None)
        for cut in near
    ]
    return near + cross


def to_other_core(values, chosen):
    return [
        move(value, ("segment",), lambda s: (s ^ 1,) if s in chosen else None) for value in values
    ]


def small_exchange(wide, narrow, mesh_f, mesh_z):
    fsdp, dp = lax.axis_size("fsdp"), lax.axis_size("dp")
    rows, channels = wide.shape
    cut = channels // (fsdp * dp)
    wide = wide.reshape(rows, fsdp, dp, cut).transpose(1, 2, 0, 3)
    narrow = jnp.broadcast_to(narrow, (fsdp, dp) + narrow.shape)
    packed = jnp.concatenate([wide, narrow], axis=3).astype(BF)
    parts = []
    for step in range(fsdp):
        part = lax.dynamic_index_in_dim(packed, (mesh_f - step) % fsdp, 0, keepdims=False)
        parts.append(rotate(part, "fsdp", -step) if step else part)
    parts = jnp.stack(parts, axis=1)
    found = []
    for step in range(dp):
        part = lax.dynamic_index_in_dim(parts, mesh_z ^ step, 0, keepdims=False)
        found.append(swap(part, "dp", step) if step else part)
    found = jnp.stack(found).reshape(-1, cut + narrow.shape[3])
    return found[:, :cut], found[:, cut:]


def on_device(inputs, cotangent, plan, weight, squeeze, excite):
    fsdp, dp = lax.axis_size("fsdp"), lax.axis_size("dp")
    sections = lax.axis_size("segment")
    section = lax.axis_index("segment")
    core, stage = section % 2, section // 2
    mesh_f, mesh_z = lax.axis_index("fsdp"), lax.axis_index("dp")
    micro, images_dev, pixels, channels = inputs.shape
    hidden = squeeze.shape[2]
    images = micro * images_dev // 2
    rows = up(images * pixels, 16)
    group = up(-(-channels // dp), 128)
    part = channels // fsdp
    tiles = [(low, min(group, channels - low)) for low in range(0, channels, group)]
    weight, squeeze, excite = weight[0], squeeze[0], excite[0]
    assert sections == 4 and dp & (dp - 1) == 0 and len(tiles) == dp
    fast = fsdp == 2 and dp % 2 == 0 and part % (2 * 16 * PIECES) == 0
    first_stage, last_stage = (0, 1), (2, 3)
    barrier = lax.optimization_barrier

    if fast:
        mine_at = mesh_f * part
        far_at = part - mine_at
        parity = mesh_z % 2
        half = part // 2
        near_at = far_at + parity * half
        cross_at = far_at + (1 - parity) * half
        pair = jnp.concatenate([squeeze, excite], axis=0)
        near_s = [parity_half(side, parity, 0, half) for side in (squeeze, excite)]
        near_s = swap(jnp.concatenate(near_s, axis=0), "fsdp")
        cross_s = swap(near_s, "dp")
        s_own = [pair, near_s, cross_s]
        s_at = [mine_at, near_at, cross_at]
        step = half // PIECES
        w_at = [mine_at] + [near_at + i * step for i in range(PIECES)]
        w_at += [cross_at + i * step for i in range(PIECES)]
    else:
        both = [lax.all_gather(side, "fsdp", axis=0, tiled=True) for side in (squeeze, excite)]
        s_own = [jnp.concatenate(both, axis=0)]
        s_at = w_at = [jnp.int32(0)]
    s_other = [swap(piece, "segment") for piece in s_own]
    n_w, n_s = len(w_at), len(s_at)

    def meta_for(at, where):
        fields = [core, (stage == where).astype(jnp.int32), mesh_f, *at]
        return jnp.stack([jnp.asarray(field, jnp.int32) for field in fields])

    slots = jnp.arange(micro, dtype=jnp.int32)
    back_order = jnp.sum(jnp.where(plan[None, :] == slots[:, None], slots[None, :], 0), axis=1)

    def flat(maps, order, send):
        maps = maps.transpose(0, 2, 1, 3).reshape(-1, channels)
        shape = ((rows, channels), BF)
        outs = [shape] + [((rows, part), BF)] * (2 * send)
        kernel = functools.partial(pick_kernel, (images, pixels, images_dev))
        smem = [meta_for([], 0), order.astype(jnp.int32)]
        return call(kernel, smem, [maps], [], outs, [], rows * channels, 4 * rows * channels)

    picked = flat(inputs, slots, fast)
    h_first = picked[0]

    saved_shapes = [
        ((rows, channels), F32),
        ((SUB, channels), F32),
        ((SUB, hidden), F32),
        ((SUB, channels), F32),
        ((SUB, hidden), F32),
    ]
    act_shape = pltpu.VMEM((rows, channels), BF)

    def weight_bufs(count, w_count):
        return [
            pltpu.VMEM((count, channels, channels), BF),
            pltpu.VMEM((2, channels, hidden), BF),
            pltpu.VMEM((2, channels, hidden), BF),
        ], [
            pltpu.SemaphoreType.DMA((count, len(tiles), w_count)),
            pltpu.SemaphoreType.DMA((2, 2, n_s)),
        ]

    def forward_pass(h_in, where, pieces):
        bufs, sems = weight_bufs(2, n_w)
        return call(
            functools.partial(forward_kernel, (n_w, n_s, images, pixels, tiles)),
            [meta_for([*w_at, *s_at], where)],
            [h_in],
            pieces,
            [((rows, channels), BF)] * 2 + saved_shapes * 2,
            [*bufs, act_shape, *sems],
            4 * rows * channels * channels,
            4 * channels * channels,
        )

    def backward_pass(d_out, saved, where, pieces, through):
        bufs, sems = weight_bufs(1 + through, n_w)
        outs = [((dp, rows, group), BF), ((SUB, hidden), F32), ((SUB, channels), F32)] * 2
        outs += [((rows, channels), BF)] * through
        return call(
            functools.partial(backward_kernel, (n_w, n_s, images, pixels, tiles, through)),
            [meta_for([*w_at, *s_at], where)],
            [d_out, *saved[0][:3], *saved[1][:3]],
            pieces,
            outs,
            [*bufs, act_shape, act_shape, *sems],
            4 * rows * channels * channels,
            4 * channels * channels,
        )

    if fast:
        w_swapped = swap(weight, "segment")
        meta_s = meta_for(s_at, 0)
        mine, give = picked[1:]
        later_weight, give = barrier((weight, give))
        far_early = far_half(later_weight, parity, last_stage)

        def share(block, mine, give):
            recv = move(
                give, ("segment", "fsdp"), lambda s, f: (s, 1 - f) if s in first_stage else None
            )
            shapes = [((rows, channels), F32), ((rows, channels), BF)]
            return recv, call(
                functools.partial(share_kernel, block),
                [meta_s],
                [mine, recv],
                [weight, w_swapped],
                shapes,
                [
                    pltpu.VMEM((2 * rows, part), BF),
                    pltpu.VMEM((part, channels), BF),
                    pltpu.SemaphoreType.DMA((len(tiles),)),
                ],
                4 * rows * part * channels,
                2 * part * channels,
            )

        def share_kernel(block, meta, mine_ref, recv_ref, own, other, *refs):
            partial_kernel((tiles,), block, meta, mine_ref, recv_ref, own, other, *refs)

        def finish(block, h_row, keep, give):
            recv = move(
                give, ("segment", "fsdp"), lambda s, f: (s, 1 - f) if s in first_stage else None
            )
            send = block == 0
            outs = [((rows, channels), BF), *saved_shapes]
            outs += [((rows, part), BF)] * (2 * send)
            return call(
                functools.partial(gate_kernel, (n_s, images, pixels, tiles, send), block),
                [meta_s],
                [h_row, keep, recv],
                [*s_own, *s_other],
                outs,
                [
                    pltpu.VMEM((channels, hidden), BF),
                    pltpu.VMEM((channels, hidden), BF),
                    act_shape,
                    pltpu.SemaphoreType.DMA((2, n_s)),
                ],
                rows * channels * 64,
                4 * channels * hidden,
            )

        d_last = flat(cotangent, back_order, False)[0]
        recv = None
        _, (keep, give) = share(0, mine, give)
        give, d_last = barrier((give, d_last))
        result = finish(0, h_first, keep, give)
        h_mid, saved_a = result[0], result[1:6]
        _, (keep, give) = share(1, *result[6:])
        late_weight, give = barrier((weight, give))
        result = finish(1, h_mid, keep, give)
        h_out, saved_b = result[0], result[1:6]
        far_late = far_half(late_weight, parity, (1,))
        late_other = to_other_core(far_late, (1,))
        early = [weight, *far_early, *s_own]
        early += [w_swapped, *to_other_core(far_early, last_stage), *s_other]
        late = [weight, *far_late, *s_own, w_swapped, *late_other, *s_other]
    else:
        d_last = flat(cotangent, back_order, False)[0]
        whole = lax.all_gather(weight, "fsdp", axis=0, tiled=True)
        early = late = [whole, *s_own, swap(whole, "segment"), *s_other]
        result = forward_pass(h_first, 0, early)
        h_mid, h_out, saved_a, saved_b = result[0], result[1], result[2:7], result[7:12]
    first = (saved_a, saved_b)

    final = stage == 1
    h_in = move(h_out, ("segment",), lambda s: (s + 2,) if s < 2 else None)
    result = forward_pass(h_in, 1, early)
    last = (result[2:7], result[7:12])
    h_a = jnp.where(final, h_in, h_first)
    h_b = jnp.where(final, result[0], h_mid)

    def swap_blocks(first, second):
        keep = jnp.where(core == 0, first, second)
        give = jnp.where(core == 0, second, first)
        return jnp.concatenate([keep, swap(give, "segment")], axis=-2)

    def of_stage(ours, theirs):
        return jnp.where(final, ours, theirs)

    h_pair = swap_blocks(h_a, h_b)
    h_mine = []
    for step in range(fsdp):
        cut = lax.dynamic_slice_in_dim(h_pair, ((mesh_f - step) % fsdp) * part, part, 1)
        h_mine.append(rotate(cut, "fsdp", -step) if step else cut)

    ended = backward_pass(d_last, last, 1, early, True)
    h_mine, ended = barrier((h_mine, ended))
    h_mine = jnp.concatenate(h_mine, axis=0)
    h_all = [h_mine] + [None] * (dp - 1)
    if dp == 4:
        h_all[1] = swap(h_mine, "dp", 1)
        h_all[2] = swap(h_mine, "dp", 2)
        inner = lax.ppermute(h_mine, "dp", [(1, 2), (2, 1)])
        outer = lax.ppermute(h_all[2], "dp", [(2, 3), (1, 0)])
        h_all[3] = jnp.where((mesh_z == 1) | (mesh_z == 2), inner, outer)
    else:
        for step in range(1, dp):
            h_all[step] = swap(h_mine, "dp", step)
    pool = swap_blocks(*[of_stage(last[b][3], first[b][3]) for b in range(2)])
    hid = swap_blocks(*[of_stage(last[b][4], first[b][4]) for b in range(2)])
    pool, hid = small_exchange(pool, hid, mesh_f, mesh_z)

    d_out = move(ended[6], ("segment",), lambda s: (s - 2,) if s > 1 else None)
    begun = backward_pass(d_out, first, 0, late, False)
    d_pre, d_sq, d_ex = [
        swap_blocks(*[of_stage(ended[3 * b + i], begun[3 * b + i]) for b in range(2)])
        for i in range(3)
    ]

    total = None
    for step in range(dp):
        piece = lax.dynamic_index_in_dim(d_pre, mesh_z ^ step, 0, keepdims=False)
        if step:
            piece = swap(piece, "dp", step)
        piece = jnp.concatenate(over_fsdp(piece), axis=0)
        term = tn(h_all[step], piece)
        total = term if total is None else total + term
    total = total.astype(BF)
    d_ex, d_sq = small_exchange(d_ex, d_sq, mesh_f, mesh_z)
    own_rows = part // dp
    gathered = jnp.zeros((dp, own_rows, group), BF)
    for step in range(dp):
        block = lax.dynamic_slice_in_dim(total, (mesh_z ^ step) * own_rows, own_rows, 0)
        if step:
            block = swap(block, "dp", step)
        gathered = lax.dynamic_update_index_in_dim(gathered, block, mesh_z ^ step, 0)
    grad_w = jnp.concatenate([gathered[i, :, :w] for i, (_, w) in enumerate(tiles)], axis=1)
    return (grad_w.astype(F32)[None], tn(pool, d_sq)[None], tn(d_ex, hid)[None])


def solution(mesh):
    placed = (
        P(None, ("fsdp", "dp"), None, None),
        P(None, ("fsdp", "dp"), None, None),
        P(),
        P("segment", "fsdp", None),
        P("segment", "fsdp", None),
        P("segment", "fsdp", None),
    )
    return jax.shard_map(
        on_device,
        mesh=mesh,
        in_specs=placed,
        out_specs=(
            P("segment", ("fsdp", "dp"), None),
            P("segment", ("fsdp", "dp"), None),
            P("segment", ("fsdp", "dp"), None),
        ),
        check_vma=False,
    )
```

```python
import functools
import itertools

import jax
import jax.numpy as jnp
from jax import lax
from jax.experimental import pallas as pl
from jax.experimental.pallas import tpu as pltpu
from jax.sharding import PartitionSpec as P

BF = jnp.bfloat16
F32 = jnp.float32
SUB = 8
PIECES = 3
VMEM_LIMIT = 62 * 1024 * 1024


def up(value, step):
    return -(-value // step) * step


def silu_slope(value):
    sigma = jax.nn.sigmoid(value)
    return sigma * (1.0 + value * (1.0 - sigma))


def nn(left, right):
    return lax.dot_general(left, right, (((1,), (0,)), ((), ())), preferred_element_type=F32)


def nt(left, right):
    return lax.dot_general(left, right, (((1,), (1,)), ((), ())), preferred_element_type=F32)


def tn(left, right):
    return lax.dot_general(left, right, (((0,), (0,)), ((), ())), preferred_element_type=F32)


class Loader:
    def __init__(self, meta, own, other, n_w, tiles):
        self.core, self.at, self.own, self.other = meta[0], meta, own, other
        self.n_w, self.tiles = n_w, tiles

    def place(self, index, rows):
        return pl.ds(pl.multiple_of(self.at[3 + index], 16), rows)

    def weight(self, refs, buf, sems, tile):
        low, width = self.tiles[tile]
        cols = pl.ds(low, width)
        for index, piece in enumerate(refs[: self.n_w]):
            target = buf.at[self.place(index, piece.shape[0]), cols]
            yield pltpu.make_async_copy(piece.at[:, cols], target, sems.at[tile, index])

    def pair(self, refs, bufs, sems):
        for index, piece in enumerate(refs[self.n_w :]):
            rows = piece.shape[0] // 2
            at = self.place(self.n_w + index, rows)
            for half, buf in enumerate(bufs):
                source = piece.at[pl.ds(half * rows, rows)]
                yield pltpu.make_async_copy(source, buf.at[at], sems.at[half, index])

    def start(self, block, kind, *args):
        for mine, refs in ((True, self.own), (False, self.other)):

            @pl.when((self.core == block) == mine)
            def _():
                for copy in kind(refs, *args):
                    copy.start()

    def wait(self, kind, *args):
        for copy in kind(self.own, *args):
            copy.wait()


def halves(value_ref, mine_ref, give_ref, index):
    part = mine_ref.shape[1]
    for here in range(value_ref.shape[1] // part):

        @pl.when(index == here)
        def _():
            mine_ref[...] = value_ref[:, here * part : (here + 1) * part]
            there = 1 - here
            give_ref[...] = value_ref[:, there * part : (there + 1) * part]


def pick_kernel(cfg, meta, order, all_ref, *refs):
    images, pixels, images_dev = cfg
    out_ref = refs[0]
    rows, count = out_ref.shape[0], all_ref.shape[0]
    per_core = images_dev // 2
    row = lax.broadcasted_iota(jnp.int32, (rows, 1), 0)
    target = jnp.full((rows, 1), -1, jnp.int32)
    for i in range(images):
        micro, slot = divmod(i, per_core)
        first = order[micro] * (pixels * images_dev) + meta[0] * per_core + slot
        inside = (row >= i * pixels) & (row < (i + 1) * pixels)
        target = jnp.where(inside, first + (row - i * pixels) * images_dev, target)
    chosen = lax.broadcasted_iota(jnp.int32, (rows, count), 1) == target
    chosen = jnp.where(chosen, 1.0, 0.0).astype(BF)
    out_ref[...] = nn(chosen, all_ref[...]).astype(BF)
    if len(refs) > 1:
        halves(out_ref, refs[1], refs[2], meta[2])


def partial_kernel(cfg, block, meta, mine_ref, recv_ref, own, other, keep_ref, give_ref, *scratch):
    (tiles,) = cfg
    x_buf, w_buf, sems = scratch
    rows = mine_ref.shape[0]

    def copy(ref, tile):
        cols = pl.ds(*tiles[tile])
        return pltpu.make_async_copy(ref.at[:, cols], w_buf.at[:, cols], sems.at[tile])

    @pl.when(meta[1] == 1)
    def _():
        for here, ref in ((True, own), (False, other)):

            @pl.when((meta[0] == block) == here)
            def _():
                for tile in range(len(tiles)):
                    copy(ref, tile).start()

        x_buf[:rows] = mine_ref[...]
        x_buf[rows:] = recv_ref[...]
        for tile, (low, width) in enumerate(tiles):
            cols = slice(low, low + width)
            copy(own, tile).wait()
            both = nn(x_buf[...], w_buf[:, cols])
            keep_ref[:, cols] = both[:rows]
            give_ref[:, cols] = both[rows:].astype(BF)


def image_masks(rows, images, pixels):
    row = lax.broadcasted_iota(jnp.int32, (rows, 1), 0)
    return [(row >= i * pixels) & (row < (i + 1) * pixels) for i in range(images)]


def per_image(value, masks):
    slot = lax.broadcasted_iota(jnp.int32, (SUB, 1), 0)
    total = jnp.zeros((SUB, value.shape[1]), F32)
    for i, mask in enumerate(masks):
        summed = jnp.sum(jnp.where(mask, value, 0.0), axis=0, keepdims=True)
        total = jnp.where(slot == i, summed, total)
    return total


def per_row(value, masks):
    spread = jnp.zeros((masks[0].shape[0], value.shape[1]), F32)
    for i, mask in enumerate(masks):
        spread = jnp.where(mask, value[i : i + 1, :], spread)
    return spread


def gated_block(tiles, masks, pixels, pre_of, src, dst, s_buf, e_buf, act_ref, outs):
    pre_ref, gate_ref, sq_ref, pool_ref, hid_ref = outs
    squeezed = jnp.zeros(sq_ref.shape, F32)
    for tile, (low, width) in enumerate(tiles):
        cols = slice(low, low + width)
        pre = pre_of(tile, cols)
        pre_ref[:, cols] = pre
        active = (pre * jax.nn.sigmoid(pre)).astype(BF)
        act_ref[:, cols] = active
        pooled = (per_image(active.astype(F32), masks) / pixels).astype(BF)
        pool_ref[:, cols] = pooled.astype(F32)
        squeezed = squeezed + nn(pooled, s_buf[cols, :])
    sq_ref[...] = squeezed
    hidden = (squeezed * jax.nn.sigmoid(squeezed)).astype(BF)
    hid_ref[...] = hidden.astype(F32)
    for low, width in tiles:
        cols = slice(low, low + width)
        gate = jax.nn.sigmoid(nt(hidden, e_buf[cols, :]))
        gate_ref[:, cols] = gate
        gated = act_ref[:, cols].astype(F32) * per_row(gate, masks)
        dst[:, cols] = (src[:, cols].astype(F32) + gated).astype(BF)


def split_pieces(refs, n_w, n_s):
    count = n_w + n_s
    return refs[:count], refs[count : 2 * count], refs[2 * count :]


def gate_kernel(cfg, block, meta, h_ref, keep_ref, recv_ref, *refs):
    n_s, images, pixels, tiles, send = cfg
    own, other, refs = split_pieces(refs, 0, n_s)
    out_ref, outs, refs = refs[0], refs[1:6], refs[6:]
    sends, refs = refs[: 2 * send], refs[2 * send :]
    s_buf, e_buf, act_ref, sems = refs
    loader = Loader(meta, own, other, 0, tiles)

    @pl.when(meta[1] == 1)
    def _():
        loader.start(block, loader.pair, (s_buf, e_buf), sems)
        masks = image_masks(h_ref.shape[0], images, pixels)
        waited = []

        def pre_of(tile, cols):
            if not waited:
                waited.append(True)
                loader.wait(loader.pair, (s_buf, e_buf), sems)
            return keep_ref[:, cols] + recv_ref[:, cols].astype(F32)

        gated_block(
            tiles, masks, pixels, pre_of, h_ref, out_ref, s_buf, e_buf, act_ref, outs
        )
        if send:
            halves(out_ref, sends[0], sends[1], meta[2])


def forward_kernel(cfg, meta, h_ref, *refs):
    n_w, n_s, images, pixels, tiles = cfg
    own, other, refs = split_pieces(refs, n_w, n_s)
    mid_ref, out_ref = refs[:2]
    outs = (refs[2:7], refs[7:12])
    w_buf, s_buf, e_buf, act_ref, w_sems, s_sems = refs[12:]
    loader = Loader(meta, own, other, n_w, tiles)

    @pl.when(meta[1] == 1)
    def _():
        for block in range(2):
            loader.start(block, loader.weight, w_buf.at[block], w_sems.at[block], 0)
            pair = (s_buf.at[block], e_buf.at[block])
            loader.start(block, loader.pair, pair, s_sems.at[block])
            for tile in range(1, len(tiles)):
                loader.start(block, loader.weight, w_buf.at[block], w_sems.at[block], tile)
        masks = image_masks(h_ref.shape[0], images, pixels)
        for block, (src, dst) in enumerate(((h_ref, mid_ref), (mid_ref, out_ref))):

            def pre_of(tile, cols):
                loader.wait(loader.weight, w_buf.at[block], w_sems.at[block], tile)
                if tile == 0:
                    pair = (s_buf.at[block], e_buf.at[block])
                    loader.wait(loader.pair, pair, s_sems.at[block])
                return nn(src[...], w_buf[block, :, cols])

            gated_block(
                tiles,
                masks,
                pixels,
                pre_of,
                src,
                dst,
                s_buf.at[block],
                e_buf.at[block],
                act_ref,
                outs[block],
            )


def backward_kernel(cfg, meta, up_ref, *refs):
    n_w, n_s, images, pixels, tiles, through = cfg
    saved, refs = (refs[:3], refs[3:6]), refs[6:]
    own, other, refs = split_pieces(refs, n_w, n_s)
    outs, refs = (refs[:3], refs[3:6]), refs[6:]
    if through:
        end_ref, refs = refs[0], refs[1:]
    w_buf, s_buf, e_buf, mid_ref, flat_ref, w_sems, s_sems = refs
    loader = Loader(meta, own, other, n_w, tiles)
    weighted = (0, 1) if through else (1,)
    slot = {block: place for place, block in enumerate(weighted)}

    @pl.when(meta[1] == 1)
    def _():
        for block in (1, 0):
            pair = (s_buf.at[block], e_buf.at[block])
            loader.start(block, loader.pair, pair, s_sems.at[block])
        for block in reversed(weighted):
            for tile in range(len(tiles)):
                at = slot[block]
                loader.start(block, loader.weight, w_buf.at[at], w_sems.at[at], tile)
        masks = image_masks(up_ref.shape[0], images, pixels)
        for block, src in ((1, up_ref), (0, mid_ref)):
            pre_ref, gate_ref, sq_ref = saved[block]
            dpre_ref, dsq_ref, dex_ref = outs[block]
            pair = (s_buf.at[block], e_buf.at[block])
            loader.wait(loader.pair, pair, s_sems.at[block])
            d_hidden = jnp.zeros(dsq_ref.shape, F32)
            for low, width in tiles:
                cols = slice(low, low + width)
                pre = pre_ref[:, cols]
                active = (pre * jax.nn.sigmoid(pre)).astype(BF).astype(F32)
                d_gate = per_image(src[:, cols].astype(F32) * active, masks)
                gate = gate_ref[:, cols]
                d_excite = (d_gate * gate * (1.0 - gate)).astype(BF)
                dex_ref[:, cols] = d_excite.astype(F32)
                d_hidden = d_hidden + nn(d_excite, e_buf[block, cols, :])
            d_squeezed = (d_hidden * silu_slope(sq_ref[...])).astype(BF)
            dsq_ref[...] = d_squeezed.astype(F32)
            for tile, (low, width) in enumerate(tiles):
                cols = slice(low, low + width)
                pre = pre_ref[:, cols]
                d_pool = nt(d_squeezed, s_buf[block, cols, :]) / pixels
                d_act = src[:, cols].astype(F32) * per_row(gate_ref[:, cols], masks)
                d_act = d_act + per_row(d_pool, masks)
                d_pre = (d_act * silu_slope(pre)).astype(BF)
                flat_ref[:, cols] = d_pre
                if width < dpre_ref.shape[2]:
                    dpre_ref[tile] = jnp.zeros(dpre_ref.shape[1:], BF)
                dpre_ref[tile, :, :width] = d_pre
            if block not in slot:
                continue
            at = slot[block]
            for tile in range(len(tiles)):
                loader.wait(loader.weight, w_buf.at[at], w_sems.at[at], tile)
            dst = mid_ref if block else end_ref
            for low, width in tiles:
                cols = slice(low, low + width)
                back = nt(flat_ref[...], w_buf[at, cols, :])
                dst[:, cols] = (src[:, cols].astype(F32) + back).astype(BF)


def call(kernel, smem, dense, pieces, outs, scratch, flops, moved):
    vmem = pl.BlockSpec(memory_space=pltpu.VMEM)
    return pl.pallas_call(
        kernel,
        out_shape=[jax.ShapeDtypeStruct(shape, dtype) for shape, dtype in outs],
        in_specs=[pl.BlockSpec(memory_space=pltpu.SMEM)] * len(smem)
        + [vmem] * len(dense)
        + [pl.BlockSpec(memory_space=pl.ANY)] * len(pieces),
        out_specs=[vmem] * len(outs),
        scratch_shapes=scratch,
        compiler_params=pltpu.CompilerParams(vmem_limit_bytes=VMEM_LIMIT),
        cost_estimate=pl.CostEstimate(flops=flops, bytes_accessed=moved, transcendentals=0),
    )(*smem, *dense, *pieces)


def move(value, axes, target):
    sizes = [lax.axis_size(axis) for axis in axes]
    pairs = []
    for index in itertools.product(*[range(size) for size in sizes]):
        goal = target(*index)
        if goal is not None:
            flat = [0, 0]
            for size, a, b in zip(sizes, index, goal):
                flat = [flat[0] * size + a, flat[1] * size + b]
            pairs.append(tuple(flat))
    return lax.ppermute(value, axes, pairs)


def swap(value, axis, stride=1):
    count = lax.axis_size(axis)
    return lax.ppermute(value, axis, [(i, i ^ stride) for i in range(count)])


def rotate(value, axis, steps):
    count = lax.axis_size(axis)
    return lax.ppermute(value, axis, [(i, (i + steps) % count) for i in range(count)])


def over_fsdp(value):
    count = lax.axis_size("fsdp")
    return [value] + [rotate(value, "fsdp", -step) for step in range(1, count)]


def parity_half(value, parity, low, rows):
    return lax.dynamic_slice_in_dim(value, parity * (value.shape[0] // 2) + low, rows, 0)


def to_other_core(values, chosen):
    return [
        move(value, ("segment",), lambda s: (s ^ 1,) if s in chosen else None) for value in values
    ]


def small_exchange(wide, narrow, mesh_f, mesh_z):
    fsdp, dp = lax.axis_size("fsdp"), lax.axis_size("dp")
    rows, channels = wide.shape
    cut = channels // (fsdp * dp)
    wide = wide.reshape(rows, fsdp, dp, cut).transpose(1, 2, 0, 3)
    narrow = jnp.broadcast_to(narrow, (fsdp, dp) + narrow.shape)
    packed = jnp.concatenate([wide, narrow], axis=3).astype(BF)
    parts = []
    for step in range(fsdp):
        part = lax.dynamic_index_in_dim(packed, (mesh_f - step) % fsdp, 0, keepdims=False)
        parts.append(rotate(part, "fsdp", -step) if step else part)
    parts = jnp.stack(parts, axis=1)
    found = []
    for step in range(dp):
        part = lax.dynamic_index_in_dim(parts, mesh_z ^ step, 0, keepdims=False)
        found.append(swap(part, "dp", step) if step else part)
    found = jnp.stack(found).reshape(-1, cut + narrow.shape[3])
    return found[:, :cut], found[:, cut:]


def on_device(inputs, cotangent, plan, weight, squeeze, excite):
    fsdp, dp = lax.axis_size("fsdp"), lax.axis_size("dp")
    sections = lax.axis_size("segment")
    section = lax.axis_index("segment")
    core, stage = section % 2, section // 2
    mesh_f, mesh_z = lax.axis_index("fsdp"), lax.axis_index("dp")
    micro, images_dev, pixels, channels = inputs.shape
    hidden = squeeze.shape[2]
    images = micro * images_dev // 2
    rows = up(images * pixels, 16)
    group = up(-(-channels // dp), 128)
    part = channels // fsdp
    tiles = [(low, min(group, channels - low)) for low in range(0, channels, group)]
    weight, squeeze, excite = weight[0], squeeze[0], excite[0]
    assert PIECES == 3 and sections == 4 and dp & (dp - 1) == 0 and len(tiles) == dp
    fast = fsdp == 2 and dp % 2 == 0 and part % (2 * 16 * PIECES) == 0
    first_stage, last_stage = (0, 1), (2, 3)
    barrier = lax.optimization_barrier

    if fast:
        mine_at = mesh_f * part
        far_at = part - mine_at
        parity = mesh_z % 2
        half = part // 2
        near_at = far_at + parity * half
        cross_at = far_at + (1 - parity) * half
        pair = jnp.concatenate([squeeze, excite], axis=0)
        near_s = [parity_half(side, parity, 0, half) for side in (squeeze, excite)]
        near_s = swap(jnp.concatenate(near_s, axis=0), "fsdp")
        cross_s = swap(near_s, "dp")
        s_own = [pair, near_s, cross_s]
        s_at = [mine_at, near_at, cross_at]
        step = half // PIECES
        w_at = [mine_at] + [near_at + i * step for i in range(PIECES)]
        w_at += [cross_at + i * step for i in range(PIECES)]
    else:
        both = [lax.all_gather(side, "fsdp", axis=0, tiled=True) for side in (squeeze, excite)]
        s_own = [jnp.concatenate(both, axis=0)]
        s_at = w_at = [jnp.int32(0)]
    s_other = [swap(piece, "segment") for piece in s_own]
    n_w, n_s = len(w_at), len(s_at)

    def meta_for(at, where):
        fields = [core, (stage == where).astype(jnp.int32), mesh_f, *at]
        return jnp.stack([jnp.asarray(field, jnp.int32) for field in fields])

    slots = jnp.arange(micro, dtype=jnp.int32)
    back_order = jnp.sum(jnp.where(plan[None, :] == slots[:, None], slots[None, :], 0), axis=1)

    def flat(maps, order, send):
        maps = maps.transpose(0, 2, 1, 3).reshape(-1, channels)
        shape = ((rows, channels), BF)
        outs = [shape] + [((rows, part), BF)] * (2 * send)
        kernel = functools.partial(pick_kernel, (images, pixels, images_dev))
        smem = [meta_for([], 0), order.astype(jnp.int32)]
        return call(kernel, smem, [maps], [], outs, [], rows * channels, 4 * rows * channels)

    picked = flat(inputs, slots, fast)
    h_first = picked[0]

    saved_shapes = [
        ((rows, channels), F32),
        ((SUB, channels), F32),
        ((SUB, hidden), F32),
        ((SUB, channels), F32),
        ((SUB, hidden), F32),
    ]
    act_shape = pltpu.VMEM((rows, channels), BF)

    def weight_bufs(count, w_count):
        return [
            pltpu.VMEM((count, channels, channels), BF),
            pltpu.VMEM((2, channels, hidden), BF),
            pltpu.VMEM((2, channels, hidden), BF),
        ], [
            pltpu.SemaphoreType.DMA((count, len(tiles), w_count)),
            pltpu.SemaphoreType.DMA((2, 2, n_s)),
        ]

    def forward_pass(h_in, where, pieces):
        bufs, sems = weight_bufs(2, n_w)
        return call(
            functools.partial(forward_kernel, (n_w, n_s, images, pixels, tiles)),
            [meta_for([*w_at, *s_at], where)],
            [h_in],
            pieces,
            [((rows, channels), BF)] * 2 + saved_shapes * 2,
            [*bufs, act_shape, *sems],
            4 * rows * channels * channels,
            4 * channels * channels,
        )

    def backward_pass(d_out, saved, where, pieces, at, through):
        bufs, sems = weight_bufs(1 + through, len(at))
        outs = [((dp, rows, group), BF), ((SUB, hidden), F32), ((SUB, channels), F32)] * 2
        outs += [((rows, channels), BF)] * through
        return call(
            functools.partial(backward_kernel, (len(at), n_s, images, pixels, tiles, through)),
            [meta_for([*at, *s_at], where)],
            [d_out, *saved[0][:3], *saved[1][:3]],
            pieces,
            outs,
            [*bufs, act_shape, act_shape, *sems],
            4 * rows * channels * channels,
            4 * channels * channels,
        )

    if fast:
        w_swapped = swap(weight, "segment")
        meta_s = meta_for(s_at, 0)
        mine, give = picked[1:]
        later_weight, give = barrier((weight, give))

        def near(index):
            cut = parity_half(later_weight, parity, index * step, step)
            return move(cut, ("segment", "fsdp"), lambda s, f: (s, 1 - f) if s > 1 else None)

        def cross(cut):
            return move(cut, ("segment", "dp"), lambda s, z: (s, z ^ 1) if s > 1 else None)

        near_w = [near(index) for index in range(PIECES)]

        def share(block, mine, give):
            recv = move(
                give, ("segment", "fsdp"), lambda s, f: (s, 1 - f) if s in first_stage else None
            )
            shapes = [((rows, channels), F32), ((rows, channels), BF)]
            return recv, call(
                functools.partial(share_kernel, block),
                [meta_s],
                [mine, recv],
                [weight, w_swapped],
                shapes,
                [
                    pltpu.VMEM((2 * rows, part), BF),
                    pltpu.VMEM((part, channels), BF),
                    pltpu.SemaphoreType.DMA((len(tiles),)),
                ],
                4 * rows * part * channels,
                2 * part * channels,
            )

        def share_kernel(block, meta, mine_ref, recv_ref, own, other, *refs):
            partial_kernel((tiles,), block, meta, mine_ref, recv_ref, own, other, *refs)

        def finish(block, h_row, keep, give):
            recv = move(
                give, ("segment", "fsdp"), lambda s, f: (s, 1 - f) if s in first_stage else None
            )
            send = block == 0
            outs = [((rows, channels), BF), *saved_shapes]
            outs += [((rows, part), BF)] * (2 * send)
            return call(
                functools.partial(gate_kernel, (n_s, images, pixels, tiles, send), block),
                [meta_s],
                [h_row, keep, recv],
                [*s_own, *s_other],
                outs,
                [
                    pltpu.VMEM((channels, hidden), BF),
                    pltpu.VMEM((channels, hidden), BF),
                    act_shape,
                    pltpu.SemaphoreType.DMA((2, n_s)),
                ],
                rows * channels * 64,
                4 * channels * hidden,
            )

        d_last = flat(cotangent, back_order, False)[0]
        mine, near_w[0] = barrier((mine, near_w[0]))
        recv_a, (keep, give) = share(0, mine, give)
        give, d_last = barrier((give, d_last))
        cross_w = [cross(near_w[0])]
        keep, cross_w[0], near_w[1] = barrier((keep, cross_w[0], near_w[1]))
        result = finish(0, h_first, keep, give)
        h_mid, saved_a = result[0], result[1:6]
        mid_mine, mid_give = result[6:]
        cross_w.append(cross(near_w[1]))
        mid_mine, cross_w[1], near_w[2] = barrier((mid_mine, cross_w[1], near_w[2]))
        recv_b, (keep, give) = share(1, mid_mine, mid_give)
        late_weight, give = barrier((weight, give))
        result = finish(1, h_mid, keep, give)
        h_out, saved_b = result[0], result[1:6]
        cross_w.append(cross(near_w[2]))
        far_early = near_w + cross_w
        far_late = [
            move(cut, ("segment", "fsdp"), lambda s, f: (s, 1 - f) if s == 1 else None)
            for cut in (late_weight[:half], late_weight[half:])
        ]
        late_other = to_other_core(far_late, (1,))
        late_at = [mine_at, far_at, far_at + half]
        early = [weight, *far_early, *s_own]
        early += [w_swapped, *to_other_core(far_early, last_stage), *s_other]
        late = [weight, *far_late, *s_own, w_swapped, *late_other, *s_other]
        first_units = [jnp.concatenate(pair, axis=0) for pair in ((mine, recv_a), (mid_mine, recv_b))]
    else:
        d_last = flat(cotangent, back_order, False)[0]
        whole = lax.all_gather(weight, "fsdp", axis=0, tiled=True)
        late_at = w_at
        early = late = [whole, *s_own, swap(whole, "segment"), *s_other]
        result = forward_pass(h_first, 0, early)
        h_mid, h_out, saved_a, saved_b = result[0], result[1], result[2:7], result[7:12]
        first_units = None
    first = (saved_a, saved_b)

    final = stage == 1

    def of_stage(ours, theirs):
        return jnp.where(final, ours, theirs)

    def fsdp_unit(value):
        found = []
        for step in range(fsdp):
            cut = lax.dynamic_slice_in_dim(value, ((mesh_f - step) % fsdp) * part, part, 1)
            if step and first_units is not None:
                cut = move(
                    cut,
                    ("segment", "fsdp"),
                    lambda s, f: (s, (f - step) % fsdp) if s > 1 else None,
                )
            elif step:
                cut = rotate(cut, "fsdp", -step)
            found.append(cut)
        return found

    def dp_slots(unit):
        found = [unit] + [swap(unit, "dp", step) for step in range(1, dp if dp != 4 else 3)]
        if dp == 4:
            inner = lax.ppermute(unit, "dp", [(1, 2), (2, 1)])
            found.append(inner)
        return found

    def forwarded(slots):
        if dp != 4:
            return slots
        outer = lax.ppermute(slots[2], "dp", [(2, 3), (1, 0)])
        return slots[:3] + [jnp.where((mesh_z == 1) | (mesh_z == 2), slots[3], outer)]

    def swap_blocks(first, second):
        keep = jnp.where(core == 0, first, second)
        give = jnp.where(core == 0, second, first)
        return keep, swap(give, "segment")

    def both_cores(first, second):
        return jnp.concatenate(swap_blocks(first, second), axis=-2)

    h_in = move(h_out, ("segment",), lambda s: (s + 2,) if s < 2 else None)
    unit_a = fsdp_unit(h_in)
    if first_units is not None:
        h_in, far_late[0] = barrier((h_in, far_late[0]))
    result = forward_pass(h_in, 1, early)
    last = (result[2:7], result[7:12])
    unit_b = fsdp_unit(result[0])
    unit_a, mid = barrier((unit_a, result[0]))
    if first_units is None:
        theirs = [jnp.concatenate(fsdp_unit(h), axis=0) for h in (h_first, h_mid)]
    else:
        theirs = first_units
    slots_a = dp_slots(of_stage(jnp.concatenate(unit_a, axis=0), theirs[0]))

    ended = backward_pass(d_last, last, 1, early, w_at, True)
    unit_b, ended = barrier((unit_b, ended))
    slots_b = dp_slots(of_stage(jnp.concatenate(unit_b, axis=0), theirs[1]))
    pool = both_cores(*[of_stage(last[b][3], first[b][3]) for b in range(2)])
    hid = both_cores(*[of_stage(last[b][4], first[b][4]) for b in range(2)])
    pool, hid = small_exchange(pool, hid, mesh_f, mesh_z)

    d_out = move(ended[6], ("segment",), lambda s: (s - 2,) if s > 1 else None)
    if dp == 4:
        d_out, slots_a[2] = barrier((d_out, slots_a[2]))
    begun = backward_pass(d_out, first, 0, late, late_at, False)
    d_pre, d_sq, d_ex = [
        both_cores(*[of_stage(ended[3 * b + i], begun[3 * b + i]) for b in range(2)])
        for i in range(3)
    ]
    h_all = []
    for slot_a, slot_b in zip(forwarded(slots_a), forwarded(slots_b)):
        keep, other = swap_blocks(slot_a, slot_b)
        cuts = []
        for step in range(fsdp):
            cuts += [side[step * rows : (step + 1) * rows] for side in (keep, other)]
        h_all.append(jnp.concatenate(cuts, axis=0))

    total = None
    for step in range(dp):
        piece = lax.dynamic_index_in_dim(d_pre, mesh_z ^ step, 0, keepdims=False)
        if step:
            piece = swap(piece, "dp", step)
        piece = jnp.concatenate(over_fsdp(piece), axis=0)
        term = tn(h_all[step], piece)
        total = term if total is None else total + term
    total = total.astype(BF)
    d_ex, d_sq = small_exchange(d_ex, d_sq, mesh_f, mesh_z)
    own_rows = part // dp
    gathered = jnp.zeros((dp, own_rows, group), BF)
    for step in range(dp):
        block = lax.dynamic_slice_in_dim(total, (mesh_z ^ step) * own_rows, own_rows, 0)
        if step:
            block = swap(block, "dp", step)
        gathered = lax.dynamic_update_index_in_dim(gathered, block, mesh_z ^ step, 0)
    grad_w = jnp.concatenate([gathered[i, :, :w] for i, (_, w) in enumerate(tiles)], axis=1)
    return (grad_w.astype(F32)[None], tn(pool, d_sq)[None], tn(d_ex, hid)[None])


def solution(mesh):
    placed = (
        P(None, ("fsdp", "dp"), None, None),
        P(None, ("fsdp", "dp"), None, None),
        P(),
        P("segment", "fsdp", None),
        P("segment", "fsdp", None),
        P("segment", "fsdp", None),
    )
    return jax.shard_map(
        on_device,
        mesh=mesh,
        in_specs=placed,
        out_specs=(
            P("segment", ("fsdp", "dp"), None),
            P("segment", ("fsdp", "dp"), None),
            P("segment", ("fsdp", "dp"), None),
        ),
        check_vma=False,
    )
```

```python
import functools
import itertools

import jax
import jax.numpy as jnp
from jax import lax
from jax.experimental import pallas as pl
from jax.experimental.pallas import tpu as pltpu
from jax.sharding import PartitionSpec as P

BF = jnp.bfloat16
F32 = jnp.float32
SUB = 8
PIECES = 3
VMEM_LIMIT = 62 * 1024 * 1024


def up(value, step):
    return -(-value // step) * step


def silu_slope(value):
    sigma = jax.nn.sigmoid(value)
    return sigma * (1.0 + value * (1.0 - sigma))


def nn(left, right):
    return lax.dot_general(left, right, (((1,), (0,)), ((), ())), preferred_element_type=F32)


def nt(left, right):
    return lax.dot_general(left, right, (((1,), (1,)), ((), ())), preferred_element_type=F32)


def tn(left, right):
    return lax.dot_general(left, right, (((0,), (0,)), ((), ())), preferred_element_type=F32)


class Loader:
    def __init__(self, meta, own, other, n_w, tiles):
        self.core, self.at, self.own, self.other = meta[0], meta, own, other
        self.n_w, self.tiles = n_w, tiles

    def place(self, index, rows):
        return pl.ds(pl.multiple_of(self.at[3 + index], 16), rows)

    def weight(self, refs, buf, sems, tile):
        low, width = self.tiles[tile]
        cols = pl.ds(low, width)
        for index, piece in enumerate(refs[: self.n_w]):
            target = buf.at[self.place(index, piece.shape[0]), cols]
            yield pltpu.make_async_copy(piece.at[:, cols], target, sems.at[tile, index])

    def pair(self, refs, bufs, sems):
        for index, piece in enumerate(refs[self.n_w :]):
            rows = piece.shape[0] // 2
            at = self.place(self.n_w + index, rows)
            for half, buf in enumerate(bufs):
                source = piece.at[pl.ds(half * rows, rows)]
                yield pltpu.make_async_copy(source, buf.at[at], sems.at[half, index])

    def start(self, block, kind, *args):
        for mine, refs in ((True, self.own), (False, self.other)):

            @pl.when((self.core == block) == mine)
            def _():
                for copy in kind(refs, *args):
                    copy.start()

    def wait(self, kind, *args):
        for copy in kind(self.own, *args):
            copy.wait()


def halves(value_ref, mine_ref, give_ref, index):
    part = mine_ref.shape[1]
    for here in range(value_ref.shape[1] // part):

        @pl.when(index == here)
        def _():
            mine_ref[...] = value_ref[:, here * part : (here + 1) * part]
            there = 1 - here
            give_ref[...] = value_ref[:, there * part : (there + 1) * part]


def pick_kernel(cfg, meta, order, all_ref, *refs):
    images, pixels, images_dev = cfg
    out_ref = refs[0]
    rows, count = out_ref.shape[0], all_ref.shape[0]
    per_core = images_dev // 2
    row = lax.broadcasted_iota(jnp.int32, (rows, 1), 0)
    target = jnp.full((rows, 1), -1, jnp.int32)
    for i in range(images):
        micro, slot = divmod(i, per_core)
        first = order[micro] * (pixels * images_dev) + meta[0] * per_core + slot
        inside = (row >= i * pixels) & (row < (i + 1) * pixels)
        target = jnp.where(inside, first + (row - i * pixels) * images_dev, target)
    chosen = lax.broadcasted_iota(jnp.int32, (rows, count), 1) == target
    chosen = jnp.where(chosen, 1.0, 0.0).astype(BF)
    out_ref[...] = nn(chosen, all_ref[...]).astype(BF)
    if len(refs) > 1:
        halves(out_ref, refs[1], refs[2], meta[2])


def partial_kernel(cfg, block, meta, mine_ref, recv_ref, own, other, keep_ref, give_ref, *scratch):
    (tiles,) = cfg
    x_buf, w_buf, sems = scratch
    rows = mine_ref.shape[0]

    def copy(ref, tile):
        cols = pl.ds(*tiles[tile])
        return pltpu.make_async_copy(ref.at[:, cols], w_buf.at[:, cols], sems.at[tile])

    @pl.when(meta[1] == 1)
    def _():
        for here, ref in ((True, own), (False, other)):

            @pl.when((meta[0] == block) == here)
            def _():
                for tile in range(len(tiles)):
                    copy(ref, tile).start()

        x_buf[:rows] = mine_ref[...]
        x_buf[rows:] = recv_ref[...]
        for tile, (low, width) in enumerate(tiles):
            cols = slice(low, low + width)
            copy(own, tile).wait()
            both = nn(x_buf[...], w_buf[:, cols])
            keep_ref[:, cols] = both[:rows]
            give_ref[:, cols] = both[rows:].astype(BF)


def image_masks(rows, images, pixels):
    row = lax.broadcasted_iota(jnp.int32, (rows, 1), 0)
    return [(row >= i * pixels) & (row < (i + 1) * pixels) for i in range(images)]


def per_image(value, masks):
    slot = lax.broadcasted_iota(jnp.int32, (SUB, 1), 0)
    total = jnp.zeros((SUB, value.shape[1]), F32)
    for i, mask in enumerate(masks):
        summed = jnp.sum(jnp.where(mask, value, 0.0), axis=0, keepdims=True)
        total = jnp.where(slot == i, summed, total)
    return total


def per_row(value, masks):
    spread = jnp.zeros((masks[0].shape[0], value.shape[1]), F32)
    for i, mask in enumerate(masks):
        spread = jnp.where(mask, value[i : i + 1, :], spread)
    return spread


def gated_block(tiles, masks, pixels, pre_of, src, dst, s_buf, e_buf, act_ref, outs):
    pre_ref, gate_ref, sq_ref, pool_ref, hid_ref = outs
    squeezed = jnp.zeros(sq_ref.shape, F32)
    for tile, (low, width) in enumerate(tiles):
        cols = slice(low, low + width)
        pre = pre_of(tile, cols)
        pre_ref[:, cols] = pre
        active = (pre * jax.nn.sigmoid(pre)).astype(BF)
        act_ref[:, cols] = active
        pooled = (per_image(active.astype(F32), masks) / pixels).astype(BF)
        pool_ref[:, cols] = pooled.astype(F32)
        squeezed = squeezed + nn(pooled, s_buf[cols, :])
    sq_ref[...] = squeezed
    hidden = (squeezed * jax.nn.sigmoid(squeezed)).astype(BF)
    hid_ref[...] = hidden.astype(F32)
    for low, width in tiles:
        cols = slice(low, low + width)
        gate = jax.nn.sigmoid(nt(hidden, e_buf[cols, :]))
        gate_ref[:, cols] = gate
        gated = act_ref[:, cols].astype(F32) * per_row(gate, masks)
        dst[:, cols] = (src[:, cols].astype(F32) + gated).astype(BF)


def split_pieces(refs, n_w, n_s):
    count = n_w + n_s
    return refs[:count], refs[count : 2 * count], refs[2 * count :]


def gate_kernel(cfg, block, meta, h_ref, keep_ref, recv_ref, *refs):
    n_s, images, pixels, tiles, send = cfg
    own, other, refs = split_pieces(refs, 0, n_s)
    out_ref, outs, refs = refs[0], refs[1:6], refs[6:]
    sends, refs = refs[: 2 * send], refs[2 * send :]
    s_buf, e_buf, act_ref, sems = refs
    loader = Loader(meta, own, other, 0, tiles)

    @pl.when(meta[1] == 1)
    def _():
        loader.start(block, loader.pair, (s_buf, e_buf), sems)
        masks = image_masks(h_ref.shape[0], images, pixels)
        waited = []

        def pre_of(tile, cols):
            if not waited:
                waited.append(True)
                loader.wait(loader.pair, (s_buf, e_buf), sems)
            return keep_ref[:, cols] + recv_ref[:, cols].astype(F32)

        gated_block(
            tiles, masks, pixels, pre_of, h_ref, out_ref, s_buf, e_buf, act_ref, outs
        )
        if send:
            halves(out_ref, sends[0], sends[1], meta[2])


def forward_kernel(cfg, meta, h_ref, *refs):
    n_w, n_s, images, pixels, tiles, send = cfg
    own, other, refs = split_pieces(refs, n_w, n_s)
    mid_ref, out_ref = refs[:2]
    outs, refs = (refs[2:7], refs[7:12]), refs[12:]
    sends, refs = refs[: 2 * send], refs[2 * send :]
    w_buf, s_buf, e_buf, act_ref, w_sems, s_sems = refs
    loader = Loader(meta, own, other, n_w, tiles)

    @pl.when(meta[1] == 1)
    def _():
        for block in range(2):
            loader.start(block, loader.weight, w_buf.at[block], w_sems.at[block], 0)
            pair = (s_buf.at[block], e_buf.at[block])
            loader.start(block, loader.pair, pair, s_sems.at[block])
            for tile in range(1, len(tiles)):
                loader.start(block, loader.weight, w_buf.at[block], w_sems.at[block], tile)
        masks = image_masks(h_ref.shape[0], images, pixels)
        for block, (src, dst) in enumerate(((h_ref, mid_ref), (mid_ref, out_ref))):

            def pre_of(tile, cols):
                loader.wait(loader.weight, w_buf.at[block], w_sems.at[block], tile)
                if tile == 0:
                    pair = (s_buf.at[block], e_buf.at[block])
                    loader.wait(loader.pair, pair, s_sems.at[block])
                return nn(src[...], w_buf[block, :, cols])

            gated_block(
                tiles,
                masks,
                pixels,
                pre_of,
                src,
                dst,
                s_buf.at[block],
                e_buf.at[block],
                act_ref,
                outs[block],
            )
            if send:
                halves(src, sends[0].at[block], sends[1].at[block], meta[2])


def backward_kernel(cfg, meta, up_ref, *refs):
    n_w, n_s, images, pixels, tiles, through = cfg
    saved, refs = (refs[:3], refs[3:6]), refs[6:]
    own, other, refs = split_pieces(refs, n_w, n_s)
    outs, refs = (refs[:3], refs[3:6]), refs[6:]
    if through:
        end_ref, refs = refs[0], refs[1:]
    w_buf, s_buf, e_buf, mid_ref, flat_ref, w_sems, s_sems = refs
    loader = Loader(meta, own, other, n_w, tiles)
    weighted = (0, 1) if through else (1,)
    slot = {block: place for place, block in enumerate(weighted)}

    @pl.when(meta[1] == 1)
    def _():
        for block in (1, 0):
            pair = (s_buf.at[block], e_buf.at[block])
            loader.start(block, loader.pair, pair, s_sems.at[block])
        for block in reversed(weighted):
            for tile in range(len(tiles)):
                at = slot[block]
                loader.start(block, loader.weight, w_buf.at[at], w_sems.at[at], tile)
        masks = image_masks(up_ref.shape[0], images, pixels)
        for block, src in ((1, up_ref), (0, mid_ref)):
            pre_ref, gate_ref, sq_ref = saved[block]
            dpre_ref, dsq_ref, dex_ref = outs[block]
            pair = (s_buf.at[block], e_buf.at[block])
            loader.wait(loader.pair, pair, s_sems.at[block])
            d_hidden = jnp.zeros(dsq_ref.shape, F32)
            for low, width in tiles:
                cols = slice(low, low + width)
                pre = pre_ref[:, cols]
                active = (pre * jax.nn.sigmoid(pre)).astype(BF).astype(F32)
                d_gate = per_image(src[:, cols].astype(F32) * active, masks)
                gate = gate_ref[:, cols]
                d_excite = (d_gate * gate * (1.0 - gate)).astype(BF)
                dex_ref[:, cols] = d_excite.astype(F32)
                d_hidden = d_hidden + nn(d_excite, e_buf[block, cols, :])
            d_squeezed = (d_hidden * silu_slope(sq_ref[...])).astype(BF)
            dsq_ref[...] = d_squeezed.astype(F32)
            for tile, (low, width) in enumerate(tiles):
                cols = slice(low, low + width)
                pre = pre_ref[:, cols]
                d_pool = nt(d_squeezed, s_buf[block, cols, :]) / pixels
                d_act = src[:, cols].astype(F32) * per_row(gate_ref[:, cols], masks)
                d_act = d_act + per_row(d_pool, masks)
                d_pre = (d_act * silu_slope(pre)).astype(BF)
                flat_ref[:, cols] = d_pre
                if width < dpre_ref.shape[2]:
                    dpre_ref[tile] = jnp.zeros(dpre_ref.shape[1:], BF)
                dpre_ref[tile, :, :width] = d_pre
            if block not in slot:
                continue
            at = slot[block]
            for tile in range(len(tiles)):
                loader.wait(loader.weight, w_buf.at[at], w_sems.at[at], tile)
            dst = mid_ref if block else end_ref
            for low, width in tiles:
                cols = slice(low, low + width)
                back = nt(flat_ref[...], w_buf[at, cols, :])
                dst[:, cols] = (src[:, cols].astype(F32) + back).astype(BF)


def call(kernel, smem, dense, pieces, outs, scratch):
    vmem = pl.BlockSpec(memory_space=pltpu.VMEM)
    return pl.pallas_call(
        kernel,
        out_shape=[jax.ShapeDtypeStruct(shape, dtype) for shape, dtype in outs],
        in_specs=[pl.BlockSpec(memory_space=pltpu.SMEM)] * len(smem)
        + [vmem] * len(dense)
        + [pl.BlockSpec(memory_space=pl.ANY)] * len(pieces),
        out_specs=[vmem] * len(outs),
        scratch_shapes=scratch,
        compiler_params=pltpu.CompilerParams(vmem_limit_bytes=VMEM_LIMIT),
        cost_estimate=pl.CostEstimate(flops=1024, bytes_accessed=1024, transcendentals=0),
    )(*smem, *dense, *pieces)


def move(value, axes, target):
    sizes = [lax.axis_size(axis) for axis in axes]
    pairs = []
    for index in itertools.product(*[range(size) for size in sizes]):
        goal = target(*index)
        if goal is not None:
            flat = [0, 0]
            for size, a, b in zip(sizes, index, goal):
                flat = [flat[0] * size + a, flat[1] * size + b]
            pairs.append(tuple(flat))
    return lax.ppermute(value, axes, pairs)


def swap(value, axis, stride=1):
    count = lax.axis_size(axis)
    return lax.ppermute(value, axis, [(i, i ^ stride) for i in range(count)])


def rotate(value, axis, steps):
    count = lax.axis_size(axis)
    return lax.ppermute(value, axis, [(i, (i + steps) % count) for i in range(count)])


def over_fsdp(value):
    count = lax.axis_size("fsdp")
    return [value] + [rotate(value, "fsdp", -step) for step in range(1, count)]


def parity_half(value, parity, low, rows):
    return lax.dynamic_slice_in_dim(value, parity * (value.shape[0] // 2) + low, rows, 0)


def to_other_core(values, chosen):
    return [
        move(value, ("segment",), lambda s: (s ^ 1,) if s in chosen else None) for value in values
    ]


def small_exchange(wides, narrow, mesh_f, mesh_z):
    fsdp, dp = lax.axis_size("fsdp"), lax.axis_size("dp")
    rows, channels = wides[0].shape
    cut = channels // (fsdp * dp)
    wides = [wide.reshape(rows, fsdp, dp, cut).transpose(1, 2, 0, 3) for wide in wides]
    narrow = jnp.broadcast_to(narrow, (fsdp, dp) + narrow.shape)
    packed = jnp.concatenate([*wides, narrow], axis=3)
    parts = []
    for step in range(fsdp):
        part = lax.dynamic_index_in_dim(packed, (mesh_f - step) % fsdp, 0, keepdims=False)
        parts.append(rotate(part, "fsdp", -step) if step else part)
    parts = jnp.stack(parts, axis=1)
    found = []
    for step in range(dp):
        part = lax.dynamic_index_in_dim(parts, mesh_z ^ step, 0, keepdims=False)
        found.append(swap(part, "dp", step) if step else part)
    found = jnp.stack(found).reshape(-1, packed.shape[3])
    return found[:, : len(wides) * cut], found[:, len(wides) * cut :]


def on_device(inputs, cotangent, plan, weight, squeeze, excite):
    fsdp, dp = lax.axis_size("fsdp"), lax.axis_size("dp")
    sections = lax.axis_size("segment")
    section = lax.axis_index("segment")
    core, stage = section % 2, section // 2
    mesh_f, mesh_z = lax.axis_index("fsdp"), lax.axis_index("dp")
    micro, images_dev, pixels, channels = inputs.shape
    hidden = squeeze.shape[2]
    images = micro * images_dev // 2
    rows = up(images * pixels, 16)
    group = up(-(-channels // dp), 128)
    part = channels // fsdp
    tiles = [(low, min(group, channels - low)) for low in range(0, channels, group)]
    weight, squeeze, excite = weight[0], squeeze[0], excite[0]
    assert PIECES == 3 and sections == 4 and dp & (dp - 1) == 0 and len(tiles) == dp
    fast = fsdp == 2 and dp % 2 == 0 and part % (2 * 16 * PIECES) == 0
    first_stage, last_stage = (0, 1), (2, 3)
    barrier = lax.optimization_barrier

    if fast:
        mine_at = mesh_f * part
        far_at = part - mine_at
        parity = mesh_z % 2
        half = part // 2
        near_at = far_at + parity * half
        cross_at = far_at + (1 - parity) * half
        near_s = [parity_half(side, parity, 0, half) for side in (squeeze, excite)]
        near_s, inputs = barrier((jnp.concatenate(near_s, axis=0), inputs))
        near_s = swap(near_s, "fsdp")
        s_at = [mine_at, near_at, cross_at]
        step = half // PIECES
        w_at = [mine_at] + [near_at + i * step for i in range(PIECES)]
        w_at += [cross_at + i * step for i in range(PIECES)]
    else:
        both = [lax.all_gather(side, "fsdp", axis=0, tiled=True) for side in (squeeze, excite)]
        s_own = [jnp.concatenate(both, axis=0)]
        s_other = [swap(s_own[0], "segment")]
        s_at = w_at = [jnp.int32(0)]
    n_w, n_s = len(w_at), len(s_at)

    def meta_for(at, where):
        fields = [core, (stage == where).astype(jnp.int32), mesh_f, *at]
        return jnp.stack([jnp.asarray(field, jnp.int32) for field in fields])

    slots = jnp.arange(micro, dtype=jnp.int32)
    back_order = jnp.sum(jnp.where(plan[None, :] == slots[:, None], slots[None, :], 0), axis=1)

    def flat(maps, order, send):
        maps = maps.transpose(0, 2, 1, 3).reshape(-1, channels)
        shape = ((rows, channels), BF)
        outs = [shape] + [((rows, part), BF)] * (2 * send)
        kernel = functools.partial(pick_kernel, (images, pixels, images_dev))
        smem = [meta_for([], 0), order.astype(jnp.int32)]
        return call(kernel, smem, [maps], [], outs, [])

    picked = flat(inputs, slots, fast)
    h_first = picked[0]

    saved_shapes = [
        ((rows, channels), F32),
        ((SUB, channels), F32),
        ((SUB, hidden), F32),
        ((SUB, channels), F32),
        ((SUB, hidden), F32),
    ]
    act_shape = pltpu.VMEM((rows, channels), BF)

    def weight_bufs(count, w_count):
        return [
            pltpu.VMEM((count, channels, channels), BF),
            pltpu.VMEM((2, channels, hidden), BF),
            pltpu.VMEM((2, channels, hidden), BF),
        ], [
            pltpu.SemaphoreType.DMA((count, len(tiles), w_count)),
            pltpu.SemaphoreType.DMA((2, 2, n_s)),
        ]

    def forward_pass(h_in, where, pieces):
        bufs, sems = weight_bufs(2, n_w)
        return call(
            functools.partial(forward_kernel, (n_w, n_s, images, pixels, tiles, fast)),
            [meta_for([*w_at, *s_at], where)],
            [h_in],
            pieces,
            [((rows, channels), BF)] * 2
            + saved_shapes * 2
            + [((2, rows, part), BF)] * (2 * fast),
            [*bufs, act_shape, *sems],
        )

    def backward_pass(d_out, saved, where, pieces, at, through):
        bufs, sems = weight_bufs(1 + through, len(at))
        outs = [((dp, rows, group), BF), ((SUB, hidden), F32), ((SUB, channels), F32)] * 2
        outs += [((rows, channels), BF)] * through
        return call(
            functools.partial(backward_kernel, (len(at), n_s, images, pixels, tiles, through)),
            [meta_for([*at, *s_at], where)],
            [d_out, *saved[0][:3], *saved[1][:3]],
            pieces,
            outs,
            [*bufs, act_shape, act_shape, *sems],
        )

    if fast:
        w_swapped = swap(weight, "segment")
        meta_s = meta_for(s_at, 0)
        mine, give = picked[1:]
        later_weight, give = barrier((weight, give))

        def near(index):
            cut = parity_half(later_weight, parity, index * step, step)
            return move(cut, ("segment", "fsdp"), lambda s, f: (s, 1 - f) if s > 1 else None)

        def cross(cut):
            return move(cut, ("segment", "dp"), lambda s, z: (s, z ^ 1) if s > 1 else None)

        near_w = [near(index) for index in range(PIECES)]

        def share(block, mine, give):
            recv = move(
                give, ("segment", "fsdp"), lambda s, f: (s, 1 - f) if s in first_stage else None
            )
            shapes = [((rows, channels), F32), ((rows, channels), BF)]
            return recv, call(
                functools.partial(share_kernel, block),
                [meta_s],
                [mine, recv],
                [weight, w_swapped],
                shapes,
                [
                    pltpu.VMEM((2 * rows, part), BF),
                    pltpu.VMEM((part, channels), BF),
                    pltpu.SemaphoreType.DMA((len(tiles),)),
                ],
            )

        def share_kernel(block, meta, mine_ref, recv_ref, own, other, *refs):
            partial_kernel((tiles,), block, meta, mine_ref, recv_ref, own, other, *refs)

        def meet(give):
            return move(
                give, ("segment", "fsdp"), lambda s, f: (s, 1 - f) if s in first_stage else None
            )

        def finish(block, h_row, keep, recv):
            send = block == 0
            outs = [((rows, channels), BF), *saved_shapes]
            outs += [((rows, part), BF)] * (2 * send)
            return call(
                functools.partial(gate_kernel, (n_s, images, pixels, tiles, send), block),
                [meta_s],
                [h_row, keep, recv],
                [*s_own, *s_other],
                outs,
                [
                    pltpu.VMEM((channels, hidden), BF),
                    pltpu.VMEM((channels, hidden), BF),
                    act_shape,
                    pltpu.SemaphoreType.DMA((2, n_s)),
                ],
            )

        mine, near_w[0] = barrier((mine, near_w[0]))
        recv_a, (keep, give) = share(0, mine, give)
        cross_w = [cross(near_w[0])]
        near_s, keep, cotangent = barrier((near_s, keep, cotangent))
        cross_s = swap(near_s, "dp")
        own_s = jnp.concatenate([squeeze, excite], axis=0)
        sides = [swap(side, "segment") for side in (squeeze, excite)]
        s_other = [jnp.concatenate(sides, axis=0)]
        s_other += [swap(near_s, "segment")]
        recv, cross_s = barrier((meet(give), cross_s))
        s_other += [swap(cross_s, "segment")]
        s_own = [own_s, near_s, cross_s]
        d_last = flat(cotangent, back_order, False)[0]
        keep, cross_w[0], near_w[1] = barrier((keep, cross_w[0], near_w[1]))
        result = finish(0, h_first, keep, recv)
        h_mid, saved_a = result[0], result[1:6]
        mid_mine, mid_give = result[6:]
        cross_w.append(cross(near_w[1]))
        mid_mine, cross_w[1], near_w[2], d_last = barrier((mid_mine, cross_w[1], near_w[2], d_last))
        recv_b, (keep, give) = share(1, mid_mine, mid_give)
        cross_w.append(cross(near_w[2]))
        result = finish(1, h_mid, keep, meet(give))
        h_out, saved_b = result[0], result[1:6]
        h_in = move(h_out, ("segment",), lambda s: (s + 2,) if s < 2 else None)
        late_weight, h_out = barrier((weight, h_out))
        far_late = [
            move(cut, ("segment", "fsdp"), lambda s, f: (s, 1 - f) if s == 1 else None)
            for cut in (late_weight[:half], late_weight[half:])
        ]
        h_in, cross_w[2] = barrier((h_in, cross_w[2]))
        far_early = near_w + cross_w
        late_at = [mine_at, far_at, far_at + half]
        early = [weight, *far_early, *s_own]
        early += [w_swapped, *to_other_core(far_early, last_stage), *s_other]
        first_units = [jnp.concatenate(pair, axis=0) for pair in ((mine, recv_a), (mid_mine, recv_b))]
    else:
        d_last = flat(cotangent, back_order, False)[0]
        whole = lax.all_gather(weight, "fsdp", axis=0, tiled=True)
        late_at = w_at
        early = late = [whole, *s_own, swap(whole, "segment"), *s_other]
        result = forward_pass(h_first, 0, early)
        h_mid, h_out, saved_a, saved_b = result[0], result[1], result[2:7], result[7:12]
        h_in = move(h_out, ("segment",), lambda s: (s + 2,) if s < 2 else None)
    first = (saved_a, saved_b)

    final = stage == 1

    def of_stage(ours, theirs):
        return jnp.where(final, ours, theirs)

    def fsdp_unit(value):
        found = []
        for step in range(fsdp):
            cut = lax.dynamic_slice_in_dim(value, ((mesh_f - step) % fsdp) * part, part, 1)
            found.append(rotate(cut, "fsdp", -step) if step else cut)
        return jnp.concatenate(found, axis=0)

    def dp_slots(unit):
        found = [unit] + [swap(unit, "dp", step) for step in range(1, dp if dp != 4 else 3)]
        if dp == 4:
            inner = lax.ppermute(unit, "dp", [(1, 2), (2, 1)])
            found.append(inner)
        return found

    def forwarded(slots):
        if dp != 4:
            return slots
        outer = lax.ppermute(slots[2], "dp", [(2, 3), (1, 0)])
        return slots[:3] + [jnp.where((mesh_z == 1) | (mesh_z == 2), slots[3], outer)]

    def swap_blocks(first, second):
        keep = jnp.where(core == 0, first, second)
        give = jnp.where(core == 0, second, first)
        return keep, swap(give, "segment")

    def both_cores(first, second):
        return jnp.concatenate(swap_blocks(first, second), axis=-2)

    result = forward_pass(h_in, 1, early)
    last = (result[2:7], result[7:12])
    if fast:
        halves_mine, halves_give = result[12:]
        halves_recv = move(
            halves_give, ("segment", "fsdp"), lambda s, f: (s, 1 - f) if s > 1 else None
        )

    ended = backward_pass(d_last, last, 1, early, w_at, True)
    d_out = move(ended[6], ("segment",), lambda s: (s - 2,) if s > 1 else None)
    if fast:
        ended = list(ended)
        halves_recv, ended[1] = barrier((halves_recv, ended[1]))
        units = [
            of_stage(jnp.concatenate([halves_mine[b], halves_recv[b]], axis=0), first_units[b])
            for b in range(2)
        ]
        late_other = to_other_core(far_late, (1,))
        late = [weight, *far_late, *s_own, w_swapped, *late_other, *s_other]
    else:
        units = [
            fsdp_unit(of_stage(ours, theirs)) for ours, theirs in ((h_in, h_first), (result[0], h_mid))
        ]
    keep, other = swap_blocks(*units)
    cuts = []
    for step in range(fsdp):
        cuts += [side[step * rows : (step + 1) * rows] for side in (keep, other)]
    h_all = dp_slots(jnp.concatenate(cuts, axis=0))

    begun = backward_pass(d_out, first, 0, late, late_at, False)
    h_all, begun = barrier((h_all, begun))
    h_all = forwarded(h_all)
    found = [
        [of_stage(ended[3 * b + i], begun[3 * b + i]) for b in range(2)] for i in range(3)
    ]
    d_pre = both_cores(*found[0])
    small = []
    for b in range(2):
        pool, hid = [of_stage(last[b][i], first[b][i]) for i in (3, 4)]
        small.append(jnp.concatenate([pool, found[2][b], hid, found[1][b]], axis=1).astype(BF))
    small = both_cores(*small)
    pool, d_ex, hid_sq = jnp.split(small, (channels, 2 * channels), axis=1)

    total = None
    for step in range(dp):
        piece = lax.dynamic_index_in_dim(d_pre, mesh_z ^ step, 0, keepdims=False)
        if step:
            piece = swap(piece, "dp", step)
        piece = jnp.concatenate(over_fsdp(piece), axis=0)
        term = tn(h_all[step], piece)
        total = term if total is None else total + term
    total = total.astype(BF)
    own_rows = part // dp
    wide, hid_sq = small_exchange([pool, d_ex], hid_sq, mesh_f, mesh_z)
    grad_s = tn(wide[:, :own_rows], hid_sq[:, hidden:])
    grad_e = tn(wide[:, own_rows:], hid_sq[:, :hidden])
    gathered = jnp.zeros((dp, own_rows, group), BF)
    for step in range(dp):
        block = lax.dynamic_slice_in_dim(total, (mesh_z ^ step) * own_rows, own_rows, 0)
        if step:
            block = swap(block, "dp", step)
        gathered = lax.dynamic_update_index_in_dim(gathered, block, mesh_z ^ step, 0)
    grad_w = jnp.concatenate([gathered[i, :, :w] for i, (_, w) in enumerate(tiles)], axis=1)
    return (grad_w.astype(F32)[None], grad_s[None], grad_e[None])


def solution(mesh):
    placed = (
        P(None, ("fsdp", "dp"), None, None),
        P(None, ("fsdp", "dp"), None, None),
        P(),
        P("segment", "fsdp", None),
        P("segment", "fsdp", None),
        P("segment", "fsdp", None),
    )
    return jax.shard_map(
        on_device,
        mesh=mesh,
        in_specs=placed,
        out_specs=(
            P("segment", ("fsdp", "dp"), None),
            P("segment", ("fsdp", "dp"), None),
            P("segment", ("fsdp", "dp"), None),
        ),
        check_vma=False,
    )
```

```python
import functools
import itertools

import jax
import jax.numpy as jnp
from jax import lax
from jax.experimental import pallas as pl
from jax.experimental.pallas import tpu as pltpu
from jax.sharding import PartitionSpec as P

BF = jnp.bfloat16
F32 = jnp.float32
SUB = 8
PIECES = 3
PASS_FLOPS = 30 * 10**9
VMEM_LIMIT = 62 * 1024 * 1024


def up(value, step):
    return -(-value // step) * step


def silu_slope(value):
    sigma = jax.nn.sigmoid(value)
    return sigma * (1.0 + value * (1.0 - sigma))


def nn(left, right):
    return lax.dot_general(left, right, (((1,), (0,)), ((), ())), preferred_element_type=F32)


def nt(left, right):
    return lax.dot_general(left, right, (((1,), (1,)), ((), ())), preferred_element_type=F32)


def tn(left, right):
    return lax.dot_general(left, right, (((0,), (0,)), ((), ())), preferred_element_type=F32)


class Loader:
    def __init__(self, meta, own, other, n_w, tiles):
        self.core, self.at, self.own, self.other = meta[0], meta, own, other
        self.n_w, self.tiles = n_w, tiles

    def place(self, index, rows):
        return pl.ds(pl.multiple_of(self.at[3 + index], 16), rows)

    def weight(self, refs, buf, sems, tile):
        low, width = self.tiles[tile]
        cols = pl.ds(low, width)
        for index, piece in enumerate(refs[: self.n_w]):
            target = buf.at[self.place(index, piece.shape[0]), cols]
            yield pltpu.make_async_copy(piece.at[:, cols], target, sems.at[tile, index])

    def pair(self, refs, bufs, sems):
        for index, piece in enumerate(refs[self.n_w :]):
            rows = piece.shape[0] // 2
            at = self.place(self.n_w + index, rows)
            for half, buf in enumerate(bufs):
                source = piece.at[pl.ds(half * rows, rows)]
                yield pltpu.make_async_copy(source, buf.at[at], sems.at[half, index])

    def start(self, block, kind, *args):
        for mine, refs in ((True, self.own), (False, self.other)):

            @pl.when((self.core == block) == mine)
            def _():
                for copy in kind(refs, *args):
                    copy.start()

    def wait(self, kind, *args):
        for copy in kind(self.own, *args):
            copy.wait()


def halves(value_ref, mine_ref, give_ref, index):
    part = mine_ref.shape[1]
    for here in range(value_ref.shape[1] // part):

        @pl.when(index == here)
        def _():
            mine_ref[...] = value_ref[:, here * part : (here + 1) * part]
            there = 1 - here
            give_ref[...] = value_ref[:, there * part : (there + 1) * part]


def pick_kernel(cfg, meta, order, all_ref, *refs):
    images, pixels, images_dev = cfg
    out_ref = refs[0]
    rows, count = out_ref.shape[0], all_ref.shape[0]
    per_core = images_dev // 2
    row = lax.broadcasted_iota(jnp.int32, (rows, 1), 0)
    target = jnp.full((rows, 1), -1, jnp.int32)
    for i in range(images):
        micro, slot = divmod(i, per_core)
        first = order[micro] * (pixels * images_dev) + meta[0] * per_core + slot
        inside = (row >= i * pixels) & (row < (i + 1) * pixels)
        target = jnp.where(inside, first + (row - i * pixels) * images_dev, target)
    chosen = lax.broadcasted_iota(jnp.int32, (rows, count), 1) == target
    chosen = jnp.where(chosen, 1.0, 0.0).astype(BF)
    out_ref[...] = nn(chosen, all_ref[...]).astype(BF)
    if len(refs) > 1:
        halves(out_ref, refs[1], refs[2], meta[2])


def partial_kernel(cfg, block, meta, mine_ref, recv_ref, own, other, keep_ref, give_ref, *scratch):
    (tiles,) = cfg
    x_buf, w_buf, sems = scratch
    rows = mine_ref.shape[0]

    def copy(ref, tile):
        cols = pl.ds(*tiles[tile])
        return pltpu.make_async_copy(ref.at[:, cols], w_buf.at[:, cols], sems.at[tile])

    @pl.when(meta[1] == 1)
    def _():
        for here, ref in ((True, own), (False, other)):

            @pl.when((meta[0] == block) == here)
            def _():
                for tile in range(len(tiles)):
                    copy(ref, tile).start()

        x_buf[:rows] = mine_ref[...]
        x_buf[rows:] = recv_ref[...]
        for tile, (low, width) in enumerate(tiles):
            cols = slice(low, low + width)
            copy(own, tile).wait()
            both = nn(x_buf[...], w_buf[:, cols])
            keep_ref[:, cols] = both[:rows]
            give_ref[:, cols] = both[rows:].astype(BF)


def image_masks(rows, images, pixels):
    row = lax.broadcasted_iota(jnp.int32, (rows, 1), 0)
    return [(row >= i * pixels) & (row < (i + 1) * pixels) for i in range(images)]


def per_image(value, masks):
    slot = lax.broadcasted_iota(jnp.int32, (SUB, 1), 0)
    total = jnp.zeros((SUB, value.shape[1]), F32)
    for i, mask in enumerate(masks):
        summed = jnp.sum(jnp.where(mask, value, 0.0), axis=0, keepdims=True)
        total = jnp.where(slot == i, summed, total)
    return total


def per_row(value, masks):
    spread = jnp.zeros((masks[0].shape[0], value.shape[1]), F32)
    for i, mask in enumerate(masks):
        spread = jnp.where(mask, value[i : i + 1, :], spread)
    return spread


def gated_block(tiles, masks, pixels, pre_of, src, dst, s_buf, e_buf, act_ref, outs):
    pre_ref, gate_ref, sq_ref, pool_ref, hid_ref = outs
    squeezed = jnp.zeros(sq_ref.shape, F32)
    for tile, (low, width) in enumerate(tiles):
        cols = slice(low, low + width)
        pre = pre_of(tile, cols)
        pre_ref[:, cols] = pre
        active = (pre * jax.nn.sigmoid(pre)).astype(BF)
        act_ref[:, cols] = active
        pooled = (per_image(active.astype(F32), masks) / pixels).astype(BF)
        pool_ref[:, cols] = pooled.astype(F32)
        squeezed = squeezed + nn(pooled, s_buf[cols, :])
    sq_ref[...] = squeezed
    hidden = (squeezed * jax.nn.sigmoid(squeezed)).astype(BF)
    hid_ref[...] = hidden.astype(F32)
    for low, width in tiles:
        cols = slice(low, low + width)
        gate = jax.nn.sigmoid(nt(hidden, e_buf[cols, :]))
        gate_ref[:, cols] = gate
        gated = act_ref[:, cols].astype(F32) * per_row(gate, masks)
        dst[:, cols] = (src[:, cols].astype(F32) + gated).astype(BF)


def split_pieces(refs, n_w, n_s):
    count = n_w + n_s
    return refs[:count], refs[count : 2 * count], refs[2 * count :]


def gate_kernel(cfg, block, meta, h_ref, keep_ref, recv_ref, *refs):
    n_s, images, pixels, tiles, send = cfg
    own, other, refs = split_pieces(refs, 0, n_s)
    out_ref, outs, refs = refs[0], refs[1:6], refs[6:]
    sends, refs = refs[: 2 * send], refs[2 * send :]
    s_buf, e_buf, act_ref, sems = refs
    loader = Loader(meta, own, other, 0, tiles)

    @pl.when(meta[1] == 1)
    def _():
        loader.start(block, loader.pair, (s_buf, e_buf), sems)
        masks = image_masks(h_ref.shape[0], images, pixels)
        waited = []

        def pre_of(tile, cols):
            if not waited:
                waited.append(True)
                loader.wait(loader.pair, (s_buf, e_buf), sems)
            return keep_ref[:, cols] + recv_ref[:, cols].astype(F32)

        gated_block(
            tiles, masks, pixels, pre_of, h_ref, out_ref, s_buf, e_buf, act_ref, outs
        )
        if send:
            halves(out_ref, sends[0], sends[1], meta[2])


def forward_kernel(cfg, meta, h_ref, *refs):
    n_w, n_s, images, pixels, tiles, send = cfg
    own, other, refs = split_pieces(refs, n_w, n_s)
    mid_ref, out_ref = refs[:2]
    outs, refs = (refs[2:7], refs[7:12]), refs[12:]
    sends, refs = refs[: 2 * send], refs[2 * send :]
    w_buf, s_buf, e_buf, act_ref, w_sems, s_sems = refs
    loader = Loader(meta, own, other, n_w, tiles)

    @pl.when(meta[1] == 1)
    def _():
        for block in range(2):
            loader.start(block, loader.weight, w_buf.at[block], w_sems.at[block], 0)
            pair = (s_buf.at[block], e_buf.at[block])
            loader.start(block, loader.pair, pair, s_sems.at[block])
            for tile in range(1, len(tiles)):
                loader.start(block, loader.weight, w_buf.at[block], w_sems.at[block], tile)
        masks = image_masks(h_ref.shape[0], images, pixels)
        for block, (src, dst) in enumerate(((h_ref, mid_ref), (mid_ref, out_ref))):

            def pre_of(tile, cols):
                loader.wait(loader.weight, w_buf.at[block], w_sems.at[block], tile)
                if tile == 0:
                    pair = (s_buf.at[block], e_buf.at[block])
                    loader.wait(loader.pair, pair, s_sems.at[block])
                return nn(src[...], w_buf[block, :, cols])

            gated_block(
                tiles,
                masks,
                pixels,
                pre_of,
                src,
                dst,
                s_buf.at[block],
                e_buf.at[block],
                act_ref,
                outs[block],
            )
            if send and block == 0:
                halves(dst, sends[0], sends[1], meta[2])


def backward_kernel(cfg, meta, up_ref, *refs):
    n_w, n_s, images, pixels, tiles, through = cfg
    saved, refs = (refs[:3], refs[3:6]), refs[6:]
    own, other, refs = split_pieces(refs, n_w, n_s)
    outs, refs = (refs[:3], refs[3:6]), refs[6:]
    if through:
        end_ref, refs = refs[0], refs[1:]
    w_buf, s_buf, e_buf, mid_ref, flat_ref, w_sems, s_sems = refs
    loader = Loader(meta, own, other, n_w, tiles)
    weighted = (0, 1) if through else (1,)
    slot = {block: place for place, block in enumerate(weighted)}

    @pl.when(meta[1] == 1)
    def _():
        for block in (1, 0):
            pair = (s_buf.at[block], e_buf.at[block])
            loader.start(block, loader.pair, pair, s_sems.at[block])
        for block in reversed(weighted):
            for tile in range(len(tiles)):
                at = slot[block]
                loader.start(block, loader.weight, w_buf.at[at], w_sems.at[at], tile)
        masks = image_masks(up_ref.shape[0], images, pixels)
        for block, src in ((1, up_ref), (0, mid_ref)):
            pre_ref, gate_ref, sq_ref = saved[block]
            dpre_ref, dsq_ref, dex_ref = outs[block]
            pair = (s_buf.at[block], e_buf.at[block])
            loader.wait(loader.pair, pair, s_sems.at[block])
            d_hidden = jnp.zeros(dsq_ref.shape, F32)
            for low, width in tiles:
                cols = slice(low, low + width)
                pre = pre_ref[:, cols]
                active = (pre * jax.nn.sigmoid(pre)).astype(BF).astype(F32)
                d_gate = per_image(src[:, cols].astype(F32) * active, masks)
                gate = gate_ref[:, cols]
                d_excite = (d_gate * gate * (1.0 - gate)).astype(BF)
                dex_ref[:, cols] = d_excite.astype(F32)
                d_hidden = d_hidden + nn(d_excite, e_buf[block, cols, :])
            d_squeezed = (d_hidden * silu_slope(sq_ref[...])).astype(BF)
            dsq_ref[...] = d_squeezed.astype(F32)
            for tile, (low, width) in enumerate(tiles):
                cols = slice(low, low + width)
                pre = pre_ref[:, cols]
                d_pool = nt(d_squeezed, s_buf[block, cols, :]) / pixels
                d_act = src[:, cols].astype(F32) * per_row(gate_ref[:, cols], masks)
                d_act = d_act + per_row(d_pool, masks)
                d_pre = (d_act * silu_slope(pre)).astype(BF)
                flat_ref[:, cols] = d_pre
                if width < dpre_ref.shape[2]:
                    dpre_ref[tile] = jnp.zeros(dpre_ref.shape[1:], BF)
                dpre_ref[tile, :, :width] = d_pre
            if block not in slot:
                continue
            at = slot[block]
            for tile in range(len(tiles)):
                loader.wait(loader.weight, w_buf.at[at], w_sems.at[at], tile)
            dst = mid_ref if block else end_ref
            for low, width in tiles:
                cols = slice(low, low + width)
                back = nt(flat_ref[...], w_buf[at, cols, :])
                dst[:, cols] = (src[:, cols].astype(F32) + back).astype(BF)


def call(kernel, smem, dense, pieces, outs, scratch, flops=1024):
    vmem = pl.BlockSpec(memory_space=pltpu.VMEM)
    return pl.pallas_call(
        kernel,
        out_shape=[jax.ShapeDtypeStruct(shape, dtype) for shape, dtype in outs],
        in_specs=[pl.BlockSpec(memory_space=pltpu.SMEM)] * len(smem)
        + [vmem] * len(dense)
        + [pl.BlockSpec(memory_space=pl.ANY)] * len(pieces),
        out_specs=[vmem] * len(outs),
        scratch_shapes=scratch,
        compiler_params=pltpu.CompilerParams(vmem_limit_bytes=VMEM_LIMIT),
        cost_estimate=pl.CostEstimate(flops=flops, bytes_accessed=1024, transcendentals=0),
    )(*smem, *dense, *pieces)


def move(value, axes, target):
    sizes = [lax.axis_size(axis) for axis in axes]
    pairs = []
    for index in itertools.product(*[range(size) for size in sizes]):
        goal = target(*index)
        if goal is not None:
            flat = [0, 0]
            for size, a, b in zip(sizes, index, goal):
                flat = [flat[0] * size + a, flat[1] * size + b]
            pairs.append(tuple(flat))
    return lax.ppermute(value, axes, pairs)


def swap(value, axis, stride=1):
    count = lax.axis_size(axis)
    return lax.ppermute(value, axis, [(i, i ^ stride) for i in range(count)])


def rotate(value, axis, steps):
    count = lax.axis_size(axis)
    return lax.ppermute(value, axis, [(i, (i + steps) % count) for i in range(count)])


def over_fsdp(value):
    count = lax.axis_size("fsdp")
    return [value] + [rotate(value, "fsdp", -step) for step in range(1, count)]


def parity_half(value, parity, low, rows):
    return lax.dynamic_slice_in_dim(value, parity * (value.shape[0] // 2) + low, rows, 0)


def to_other_core(values, chosen):
    return [
        move(value, ("segment",), lambda s: (s ^ 1,) if s in chosen else None) for value in values
    ]


def small_exchange(wides, narrow, mesh_f, mesh_z):
    fsdp, dp = lax.axis_size("fsdp"), lax.axis_size("dp")
    rows, channels = wides[0].shape
    cut = channels // (fsdp * dp)
    wides = [wide.reshape(rows, fsdp, dp, cut).transpose(1, 2, 0, 3) for wide in wides]
    narrow = jnp.broadcast_to(narrow, (fsdp, dp) + narrow.shape)
    packed = jnp.concatenate([*wides, narrow], axis=3)
    parts = []
    for step in range(fsdp):
        part = lax.dynamic_index_in_dim(packed, (mesh_f - step) % fsdp, 0, keepdims=False)
        parts.append(rotate(part, "fsdp", -step) if step else part)
    parts = jnp.stack(parts, axis=1)
    found = []
    for step in range(dp):
        part = lax.dynamic_index_in_dim(parts, mesh_z ^ step, 0, keepdims=False)
        found.append(swap(part, "dp", step) if step else part)
    found = jnp.stack(found).reshape(-1, packed.shape[3])
    return found[:, : len(wides) * cut], found[:, len(wides) * cut :]


def on_device(inputs, cotangent, plan, weight, squeeze, excite):
    fsdp, dp = lax.axis_size("fsdp"), lax.axis_size("dp")
    sections = lax.axis_size("segment")
    section = lax.axis_index("segment")
    core, stage = section % 2, section // 2
    mesh_f, mesh_z = lax.axis_index("fsdp"), lax.axis_index("dp")
    micro, images_dev, pixels, channels = inputs.shape
    hidden = squeeze.shape[2]
    images = micro * images_dev // 2
    rows = up(images * pixels, 16)
    group = up(-(-channels // dp), 128)
    part = channels // fsdp
    tiles = [(low, min(group, channels - low)) for low in range(0, channels, group)]
    weight, squeeze, excite = weight[0], squeeze[0], excite[0]
    assert PIECES == 3 and sections == 4 and dp & (dp - 1) == 0 and len(tiles) == dp
    fast = fsdp == 2 and dp % 2 == 0 and part % (2 * 16 * PIECES) == 0
    first_stage, last_stage = (0, 1), (2, 3)
    barrier = lax.optimization_barrier

    if fast:
        mine_at = mesh_f * part
        far_at = part - mine_at
        parity = mesh_z % 2
        half = part // 2
        near_at = far_at + parity * half
        cross_at = far_at + (1 - parity) * half
        near_s = [parity_half(side, parity, 0, half) for side in (squeeze, excite)]
        near_cut, inputs = barrier((jnp.concatenate(near_s, axis=0), inputs))
        s_at = [mine_at, near_at, cross_at]
        step = half // PIECES
        w_at = [mine_at] + [near_at + i * step for i in range(PIECES)]
        w_at += [cross_at + i * step for i in range(PIECES)]
    else:
        both = [lax.all_gather(side, "fsdp", axis=0, tiled=True) for side in (squeeze, excite)]
        s_own = [jnp.concatenate(both, axis=0)]
        s_other = [swap(s_own[0], "segment")]
        s_at = w_at = [jnp.int32(0)]
    n_w, n_s = len(w_at), len(s_at)

    def meta_for(at, where):
        fields = [core, (stage == where).astype(jnp.int32), mesh_f, *at]
        return jnp.stack([jnp.asarray(field, jnp.int32) for field in fields])

    slots = jnp.arange(micro, dtype=jnp.int32)
    back_order = jnp.sum(jnp.where(plan[None, :] == slots[:, None], slots[None, :], 0), axis=1)

    def flat(maps, order, send):
        maps = maps.transpose(0, 2, 1, 3).reshape(-1, channels)
        shape = ((rows, channels), BF)
        outs = [shape] + [((rows, part), BF)] * (2 * send)
        kernel = functools.partial(pick_kernel, (images, pixels, images_dev))
        smem = [meta_for([], 0), order.astype(jnp.int32)]
        return call(kernel, smem, [maps], [], outs, [])

    picked = flat(inputs, slots, fast)
    h_first = picked[0]

    saved_shapes = [
        ((rows, channels), F32),
        ((SUB, channels), F32),
        ((SUB, hidden), F32),
        ((SUB, channels), F32),
        ((SUB, hidden), F32),
    ]
    act_shape = pltpu.VMEM((rows, channels), BF)

    def weight_bufs(count, w_count):
        return [
            pltpu.VMEM((count, channels, channels), BF),
            pltpu.VMEM((2, channels, hidden), BF),
            pltpu.VMEM((2, channels, hidden), BF),
        ], [
            pltpu.SemaphoreType.DMA((count, len(tiles), w_count)),
            pltpu.SemaphoreType.DMA((2, 2, n_s)),
        ]

    def forward_pass(h_in, where, pieces):
        bufs, sems = weight_bufs(2, n_w)
        return call(
            functools.partial(forward_kernel, (n_w, n_s, images, pixels, tiles, fast)),
            [meta_for([*w_at, *s_at], where)],
            [h_in],
            pieces,
            [((rows, channels), BF)] * 2
            + saved_shapes * 2
            + [((rows, part), BF)] * (2 * fast),
            [*bufs, act_shape, *sems],
            PASS_FLOPS,
        )

    def backward_pass(d_out, saved, where, pieces, at, through):
        bufs, sems = weight_bufs(1 + through, len(at))
        outs = [((dp, rows, group), BF), ((SUB, hidden), F32), ((SUB, channels), F32)] * 2
        outs += [((rows, channels), BF)] * through
        return call(
            functools.partial(backward_kernel, (len(at), n_s, images, pixels, tiles, through)),
            [meta_for([*at, *s_at], where)],
            [d_out, *saved[0][:3], *saved[1][:3]],
            pieces,
            outs,
            [*bufs, act_shape, act_shape, *sems],
            PASS_FLOPS if through else 1024,
        )

    if fast:
        w_swapped = swap(weight, "segment")
        meta_s = meta_for(s_at, 0)
        mine, give = picked[1:]
        later_weight, give = barrier((weight, give))

        def near(index):
            cut = parity_half(later_weight, parity, index * step, step)
            return move(cut, ("segment", "fsdp"), lambda s, f: (s, 1 - f) if s > 1 else None)

        def cross(cut):
            return move(cut, ("segment", "dp"), lambda s, z: (s, z ^ 1) if s > 1 else None)

        near_w = [near(index) for index in range(PIECES)]

        def meet(give):
            return move(
                give, ("segment", "fsdp"), lambda s, f: (s, 1 - f) if s in first_stage else None
            )

        def share(block, mine, recv):
            shapes = [((rows, channels), F32), ((rows, channels), BF)]
            return call(
                functools.partial(share_kernel, block),
                [meta_s],
                [mine, recv],
                [weight, w_swapped],
                shapes,
                [
                    pltpu.VMEM((2 * rows, part), BF),
                    pltpu.VMEM((part, channels), BF),
                    pltpu.SemaphoreType.DMA((len(tiles),)),
                ],
            )

        def share_kernel(block, meta, mine_ref, recv_ref, own, other, *refs):
            partial_kernel((tiles,), block, meta, mine_ref, recv_ref, own, other, *refs)

        def finish(block, h_row, keep, recv):
            send = True
            outs = [((rows, channels), BF), *saved_shapes]
            outs += [((rows, part), BF)] * (2 * send)
            return call(
                functools.partial(gate_kernel, (n_s, images, pixels, tiles, send), block),
                [meta_s],
                [h_row, keep, recv],
                [*s_own, *s_other],
                outs,
                [
                    pltpu.VMEM((channels, hidden), BF),
                    pltpu.VMEM((channels, hidden), BF),
                    act_shape,
                    pltpu.SemaphoreType.DMA((2, n_s)),
                ],
            )

        recv_a, near_cut = barrier((meet(give), near_cut))
        near_s = swap(near_cut, "fsdp")
        own_s = jnp.concatenate([squeeze, excite], axis=0)
        other_s = jnp.concatenate([swap(side, "segment") for side in (squeeze, excite)], axis=0)
        mine, near_w[0], own_s, other_s = barrier((mine, near_w[0], own_s, other_s))
        keep, give = share(0, mine, recv_a)
        cross_w = [cross(near_w[0])]
        near_s, keep, cotangent = barrier((near_s, keep, cotangent))
        cross_s = swap(near_s, "dp")
        recv, cross_s = barrier((meet(give), cross_s))
        s_other = [other_s, swap(near_s, "segment"), swap(cross_s, "segment")]
        s_own = [own_s, near_s, cross_s]
        d_last = flat(cotangent, back_order, False)[0]
        keep, cross_w[0], *near_w[1:] = barrier((keep, cross_w[0], *near_w[1:]))
        result = finish(0, h_first, keep, recv)
        h_mid, saved_a = result[0], result[1:6]
        mid_mine, mid_give = result[6:]
        cross_w.append(cross(near_w[1]))
        cross_w.append(cross(near_w[2]))
        recv_b = meet(mid_give)
        mid_mine, cross_w[1], d_last = barrier((mid_mine, cross_w[1], d_last))
        keep, give = share(1, mid_mine, recv_b)
        result = finish(1, h_mid, keep, meet(give))
        h_out, saved_b = result[0], result[1:6]
        out_mine, out_give = result[6:]
        h_in = move(h_out, ("segment",), lambda s: (s + 2,) if s < 2 else None)
        in_recv = move(
            out_give, ("segment", "fsdp"), lambda s, f: (s + 2, 1 - f) if s < 2 else None
        )
        late_weight, h_out = barrier((weight, h_out))
        far_late = [
            move(cut, ("segment", "fsdp"), lambda s, f: (s, 1 - f) if s == 1 else None)
            for cut in (late_weight[:half], late_weight[half:])
        ]
        h_in, cross_w[2] = barrier((h_in, cross_w[2]))
        far_early = near_w + cross_w
        late_at = [mine_at, far_at, far_at + half]
        early = [weight, *far_early, *s_own]
        early += [w_swapped, *to_other_core(far_early, last_stage), *s_other]
        first_units = [jnp.concatenate(pair, axis=0) for pair in ((mine, recv_a), (mid_mine, recv_b))]
    else:
        d_last = flat(cotangent, back_order, False)[0]
        whole = lax.all_gather(weight, "fsdp", axis=0, tiled=True)
        late_at = w_at
        early = late = [whole, *s_own, swap(whole, "segment"), *s_other]
        result = forward_pass(h_first, 0, early)
        h_mid, h_out, saved_a, saved_b = result[0], result[1], result[2:7], result[7:12]
        h_in = move(h_out, ("segment",), lambda s: (s + 2,) if s < 2 else None)
    first = (saved_a, saved_b)

    final = stage == 1

    def of_stage(ours, theirs):
        return jnp.where(final, ours, theirs)

    def fsdp_unit(value):
        found = []
        for step in range(fsdp):
            cut = lax.dynamic_slice_in_dim(value, ((mesh_f - step) % fsdp) * part, part, 1)
            found.append(rotate(cut, "fsdp", -step) if step else cut)
        return jnp.concatenate(found, axis=0)

    def dp_slots(unit):
        found = [unit] + [swap(unit, "dp", step) for step in range(1, dp if dp != 4 else 3)]
        if dp == 4:
            inner = lax.ppermute(unit, "dp", [(1, 2), (2, 1)])
            found.append(inner)
        return found

    def forwarded(slots):
        if dp != 4:
            return slots
        outer = lax.ppermute(slots[2], "dp", [(2, 3), (1, 0)])
        return slots[:3] + [jnp.where((mesh_z == 1) | (mesh_z == 2), slots[3], outer)]

    def swap_blocks(first, second):
        keep = jnp.where(core == 0, first, second)
        give = jnp.where(core == 0, second, first)
        return keep, swap(give, "segment")

    def both_cores(first, second):
        return jnp.concatenate(swap_blocks(first, second), axis=-2)

    if fast:
        in_mine = jnp.where(mesh_f == 0, h_in[:, :part], h_in[:, part:])
        unit = of_stage(jnp.concatenate([in_mine, in_recv], axis=0), first_units[0])
    else:
        unit = fsdp_unit(of_stage(h_in, h_first))
    h_in, unit = barrier((h_in, unit))
    slots_a = dp_slots(unit)
    result = forward_pass(h_in, 1, early)
    result, slots_a, d_last = barrier((list(result), slots_a, d_last))
    last = (result[2:7], result[7:12])
    if fast:
        mid_recv = move(
            result[13], ("segment", "fsdp"), lambda s, f: (s, 1 - f) if s > 1 else None
        )

    ended = list(backward_pass(d_last, last, 1, early, w_at, True))
    d_out = move(ended[6], ("segment",), lambda s: (s - 2,) if s > 1 else None)
    if fast:
        mid_recv, far_late, ended[1] = barrier((mid_recv, far_late, ended[1]))
        ours = jnp.concatenate([result[12], mid_recv], axis=0)
        unit = of_stage(ours, first_units[1])
        late_other = to_other_core(far_late, (1,))
        late = [weight, *far_late, *s_own, w_swapped, *late_other, *s_other]
    else:
        unit = fsdp_unit(of_stage(result[0], h_mid))
    slots_b = dp_slots(unit)
    slots_a = forwarded(slots_a)

    begun = backward_pass(d_out, first, 0, late, late_at, False)
    slots_b, begun = barrier((slots_b, begun))
    slots_b = forwarded(slots_b)
    h_all = []
    for slot_a, slot_b in zip(slots_a, slots_b):
        keep, other = swap_blocks(slot_a, slot_b)
        cuts = []
        for step in range(fsdp):
            cuts += [side[step * rows : (step + 1) * rows] for side in (keep, other)]
        h_all.append(jnp.concatenate(cuts, axis=0))
    found = [
        [of_stage(ended[3 * b + i], begun[3 * b + i]) for b in range(2)] for i in range(3)
    ]
    d_pre = both_cores(*found[0])
    small = []
    for b in range(2):
        pool, hid = [of_stage(last[b][i], first[b][i]) for i in (3, 4)]
        small.append(jnp.concatenate([pool, found[2][b], hid, found[1][b]], axis=1).astype(BF))
    small = both_cores(*small)
    pool, d_ex, hid_sq = jnp.split(small, (channels, 2 * channels), axis=1)

    total = None
    for step in range(dp):
        piece = lax.dynamic_index_in_dim(d_pre, mesh_z ^ step, 0, keepdims=False)
        if step:
            piece = swap(piece, "dp", step)
        piece = jnp.concatenate(over_fsdp(piece), axis=0)
        term = tn(h_all[step], piece)
        total = term if total is None else total + term
    total = total.astype(BF)
    own_rows = part // dp
    wide, hid_sq = small_exchange([pool, d_ex], hid_sq, mesh_f, mesh_z)
    grad_s = tn(wide[:, :own_rows], hid_sq[:, hidden:])
    grad_e = tn(wide[:, own_rows:], hid_sq[:, :hidden])
    gathered = jnp.zeros((dp, own_rows, group), BF)
    for step in range(dp):
        block = lax.dynamic_slice_in_dim(total, (mesh_z ^ step) * own_rows, own_rows, 0)
        if step:
            block = swap(block, "dp", step)
        gathered = lax.dynamic_update_index_in_dim(gathered, block, mesh_z ^ step, 0)
    grad_w = jnp.concatenate([gathered[i, :, :w] for i, (_, w) in enumerate(tiles)], axis=1)
    return (grad_w.astype(F32)[None], grad_s[None], grad_e[None])


def solution(mesh):
    placed = (
        P(None, ("fsdp", "dp"), None, None),
        P(None, ("fsdp", "dp"), None, None),
        P(),
        P("segment", "fsdp", None),
        P("segment", "fsdp", None),
        P("segment", "fsdp", None),
    )
    return jax.shard_map(
        on_device,
        mesh=mesh,
        in_specs=placed,
        out_specs=(
            P("segment", ("fsdp", "dp"), None),
            P("segment", ("fsdp", "dp"), None),
            P("segment", ("fsdp", "dp"), None),
        ),
        check_vma=False,
    )
```

```python
import functools
import itertools

import jax
import jax.numpy as jnp
from jax import lax
from jax.experimental import pallas as pl
from jax.experimental.pallas import tpu as pltpu
from jax.sharding import PartitionSpec as P

BF = jnp.bfloat16
F32 = jnp.float32
SUB = 8
PASS_FLOPS = 30 * 10**9
VMEM_LIMIT = 62 * 1024 * 1024


def up(value, step):
    return -(-value // step) * step


def silu_slope(value):
    sigma = jax.nn.sigmoid(value)
    return sigma * (1.0 + value * (1.0 - sigma))


def nn(left, right):
    return lax.dot_general(left, right, (((1,), (0,)), ((), ())), preferred_element_type=F32)


def nt(left, right):
    return lax.dot_general(left, right, (((1,), (1,)), ((), ())), preferred_element_type=F32)


def tn(left, right):
    return lax.dot_general(left, right, (((0,), (0,)), ((), ())), preferred_element_type=F32)


class Loader:
    def __init__(self, meta, own, other, n_w, tiles):
        self.core, self.at, self.own, self.other = meta[0], meta, own, other
        self.n_w, self.tiles = n_w, tiles

    def place(self, index, rows):
        return pl.ds(pl.multiple_of(self.at[3 + index], 16), rows)

    def weight(self, refs, buf, sems, tile):
        low, width = self.tiles[tile]
        cols = pl.ds(low, width)
        for index, piece in enumerate(refs[: self.n_w]):
            target = buf.at[self.place(index, piece.shape[0]), cols]
            yield pltpu.make_async_copy(piece.at[:, cols], target, sems.at[tile, index])

    def pair(self, refs, bufs, sems):
        for index, piece in enumerate(refs[self.n_w :]):
            rows = piece.shape[0] // 2
            at = self.place(self.n_w + index, rows)
            for half, buf in enumerate(bufs):
                source = piece.at[pl.ds(half * rows, rows)]
                yield pltpu.make_async_copy(source, buf.at[at], sems.at[half, index])

    def start(self, block, kind, *args):
        for mine, refs in ((True, self.own), (False, self.other)):

            @pl.when((self.core == block) == mine)
            def _():
                for copy in kind(refs, *args):
                    copy.start()

    def wait(self, kind, *args):
        for copy in kind(self.own, *args):
            copy.wait()


def halves(value_ref, mine_ref, give_ref, index):
    part = mine_ref.shape[1]
    for here in range(value_ref.shape[1] // part):

        @pl.when(index == here)
        def _():
            mine_ref[...] = value_ref[:, here * part : (here + 1) * part]
            there = 1 - here
            give_ref[...] = value_ref[:, there * part : (there + 1) * part]


def pick_kernel(cfg, meta, order, all_ref, *refs):
    images, pixels, images_dev = cfg
    out_ref = refs[0]
    rows, count = out_ref.shape[0], all_ref.shape[0]
    per_core = images_dev // 2
    row = lax.broadcasted_iota(jnp.int32, (rows, 1), 0)
    target = jnp.full((rows, 1), -1, jnp.int32)
    for i in range(images):
        micro, slot = divmod(i, per_core)
        first = order[micro] * (pixels * images_dev) + meta[0] * per_core + slot
        inside = (row >= i * pixels) & (row < (i + 1) * pixels)
        target = jnp.where(inside, first + (row - i * pixels) * images_dev, target)
    chosen = lax.broadcasted_iota(jnp.int32, (rows, count), 1) == target
    chosen = jnp.where(chosen, 1.0, 0.0).astype(BF)
    out_ref[...] = nn(chosen, all_ref[...]).astype(BF)
    if len(refs) > 1:
        halves(out_ref, refs[1], refs[2], meta[2])


def partial_kernel(cfg, block, meta, mine_ref, recv_ref, own, other, keep_ref, give_ref, *scratch):
    (tiles,) = cfg
    x_buf, w_buf, sems = scratch
    rows = mine_ref.shape[0]

    def copy(ref, tile):
        cols = pl.ds(*tiles[tile])
        return pltpu.make_async_copy(ref.at[:, cols], w_buf.at[:, cols], sems.at[tile])

    @pl.when(meta[1] == 1)
    def _():
        for here, ref in ((True, own), (False, other)):

            @pl.when((meta[0] == block) == here)
            def _():
                for tile in range(len(tiles)):
                    copy(ref, tile).start()

        x_buf[:rows] = mine_ref[...]
        x_buf[rows:] = recv_ref[...]
        for tile, (low, width) in enumerate(tiles):
            cols = slice(low, low + width)
            copy(own, tile).wait()
            both = nn(x_buf[...], w_buf[:, cols])
            keep_ref[:, cols] = both[:rows]
            give_ref[:, cols] = both[rows:].astype(BF)


def image_masks(rows, images, pixels):
    row = lax.broadcasted_iota(jnp.int32, (rows, 1), 0)
    return [(row >= i * pixels) & (row < (i + 1) * pixels) for i in range(images)]


def per_image(value, masks):
    slot = lax.broadcasted_iota(jnp.int32, (SUB, 1), 0)
    total = jnp.zeros((SUB, value.shape[1]), F32)
    for i, mask in enumerate(masks):
        summed = jnp.sum(jnp.where(mask, value, 0.0), axis=0, keepdims=True)
        total = jnp.where(slot == i, summed, total)
    return total


def per_row(value, masks):
    spread = jnp.zeros((masks[0].shape[0], value.shape[1]), F32)
    for i, mask in enumerate(masks):
        spread = jnp.where(mask, value[i : i + 1, :], spread)
    return spread


def gated_block(tiles, masks, pixels, pre_of, src, dst, s_buf, e_buf, act_ref, outs):
    pre_ref, gate_ref, sq_ref, pool_ref, hid_ref = outs
    squeezed = jnp.zeros(sq_ref.shape, F32)
    for tile, (low, width) in enumerate(tiles):
        cols = slice(low, low + width)
        pre = pre_of(tile, cols)
        pre_ref[:, cols] = pre
        active = (pre * jax.nn.sigmoid(pre)).astype(BF)
        act_ref[:, cols] = active
        pooled = (per_image(active.astype(F32), masks) / pixels).astype(BF)
        pool_ref[:, cols] = pooled.astype(F32)
        squeezed = squeezed + nn(pooled, s_buf[cols, :])
    sq_ref[...] = squeezed
    hidden = (squeezed * jax.nn.sigmoid(squeezed)).astype(BF)
    hid_ref[...] = hidden.astype(F32)
    for low, width in tiles:
        cols = slice(low, low + width)
        gate = jax.nn.sigmoid(nt(hidden, e_buf[cols, :]))
        gate_ref[:, cols] = gate
        gated = act_ref[:, cols].astype(F32) * per_row(gate, masks)
        dst[:, cols] = (src[:, cols].astype(F32) + gated).astype(BF)


def split_pieces(refs, n_w, n_s):
    count = n_w + n_s
    return refs[:count], refs[count : 2 * count], refs[2 * count :]


def gate_kernel(cfg, block, meta, h_ref, keep_ref, recv_ref, *refs):
    n_s, images, pixels, tiles, send = cfg
    own, other, refs = split_pieces(refs, 0, n_s)
    out_ref, outs, refs = refs[0], refs[1:6], refs[6:]
    sends, refs = refs[: 2 * send], refs[2 * send :]
    s_buf, e_buf, act_ref, sems = refs
    loader = Loader(meta, own, other, 0, tiles)

    @pl.when(meta[1] == 1)
    def _():
        loader.start(block, loader.pair, (s_buf, e_buf), sems)
        masks = image_masks(h_ref.shape[0], images, pixels)
        waited = []

        def pre_of(tile, cols):
            if not waited:
                waited.append(True)
                loader.wait(loader.pair, (s_buf, e_buf), sems)
            return keep_ref[:, cols] + recv_ref[:, cols].astype(F32)

        gated_block(
            tiles, masks, pixels, pre_of, h_ref, out_ref, s_buf, e_buf, act_ref, outs
        )
        if send:
            halves(out_ref, sends[0], sends[1], meta[2])


def forward_kernel(cfg, meta, h_ref, *refs):
    n_w, n_s, images, pixels, tiles, send = cfg
    own, other, refs = split_pieces(refs, n_w, n_s)
    mid_ref, out_ref = refs[:2]
    outs, refs = (refs[2:7], refs[7:12]), refs[12:]
    sends, refs = refs[: 2 * send], refs[2 * send :]
    w_buf, s_buf, e_buf, act_ref, w_sems, s_sems = refs
    loader = Loader(meta, own, other, n_w, tiles)

    @pl.when(meta[1] == 1)
    def _():
        for block in range(2):
            loader.start(block, loader.weight, w_buf.at[block], w_sems.at[block], 0)
            pair = (s_buf.at[block], e_buf.at[block])
            loader.start(block, loader.pair, pair, s_sems.at[block])
            for tile in range(1, len(tiles)):
                loader.start(block, loader.weight, w_buf.at[block], w_sems.at[block], tile)
        masks = image_masks(h_ref.shape[0], images, pixels)
        for block, (src, dst) in enumerate(((h_ref, mid_ref), (mid_ref, out_ref))):

            def pre_of(tile, cols):
                loader.wait(loader.weight, w_buf.at[block], w_sems.at[block], tile)
                if tile == 0:
                    pair = (s_buf.at[block], e_buf.at[block])
                    loader.wait(loader.pair, pair, s_sems.at[block])
                return nn(src[...], w_buf[block, :, cols])

            gated_block(
                tiles,
                masks,
                pixels,
                pre_of,
                src,
                dst,
                s_buf.at[block],
                e_buf.at[block],
                act_ref,
                outs[block],
            )
            if send and block == 0:
                halves(dst, sends[0], sends[1], meta[2])


def backward_kernel(cfg, meta, up_ref, *refs):
    n_w, n_s, images, pixels, tiles, through = cfg
    saved, refs = (refs[:3], refs[3:6]), refs[6:]
    own, other, refs = split_pieces(refs, n_w, n_s)
    outs, refs = (refs[:3], refs[3:6]), refs[6:]
    if through:
        end_ref, refs = refs[0], refs[1:]
    w_buf, s_buf, e_buf, mid_ref, flat_ref, w_sems, s_sems = refs
    loader = Loader(meta, own, other, n_w, tiles)
    weighted = (0, 1) if through else (1,)
    slot = {block: place for place, block in enumerate(weighted)}

    @pl.when(meta[1] == 1)
    def _():
        for block in (1, 0):
            pair = (s_buf.at[block], e_buf.at[block])
            loader.start(block, loader.pair, pair, s_sems.at[block])
        for block in reversed(weighted):
            for tile in range(len(tiles)):
                at = slot[block]
                loader.start(block, loader.weight, w_buf.at[at], w_sems.at[at], tile)
        masks = image_masks(up_ref.shape[0], images, pixels)
        for block, src in ((1, up_ref), (0, mid_ref)):
            pre_ref, gate_ref, sq_ref = saved[block]
            dpre_ref, dsq_ref, dex_ref = outs[block]
            pair = (s_buf.at[block], e_buf.at[block])
            loader.wait(loader.pair, pair, s_sems.at[block])
            d_hidden = jnp.zeros(dsq_ref.shape, F32)
            for low, width in tiles:
                cols = slice(low, low + width)
                pre = pre_ref[:, cols]
                active = (pre * jax.nn.sigmoid(pre)).astype(BF).astype(F32)
                d_gate = per_image(src[:, cols].astype(F32) * active, masks)
                gate = gate_ref[:, cols]
                d_excite = (d_gate * gate * (1.0 - gate)).astype(BF)
                dex_ref[:, cols] = d_excite.astype(F32)
                d_hidden = d_hidden + nn(d_excite, e_buf[block, cols, :])
            d_squeezed = (d_hidden * silu_slope(sq_ref[...])).astype(BF)
            dsq_ref[...] = d_squeezed.astype(F32)
            for tile, (low, width) in enumerate(tiles):
                cols = slice(low, low + width)
                pre = pre_ref[:, cols]
                d_pool = nt(d_squeezed, s_buf[block, cols, :]) / pixels
                d_act = src[:, cols].astype(F32) * per_row(gate_ref[:, cols], masks)
                d_act = d_act + per_row(d_pool, masks)
                d_pre = (d_act * silu_slope(pre)).astype(BF)
                flat_ref[:, cols] = d_pre
                if width < dpre_ref.shape[2]:
                    dpre_ref[tile] = jnp.zeros(dpre_ref.shape[1:], BF)
                dpre_ref[tile, :, :width] = d_pre
            if block not in slot:
                continue
            at = slot[block]
            for tile in range(len(tiles)):
                loader.wait(loader.weight, w_buf.at[at], w_sems.at[at], tile)
            dst = mid_ref if block else end_ref
            for low, width in tiles:
                cols = slice(low, low + width)
                back = nt(flat_ref[...], w_buf[at, cols, :])
                dst[:, cols] = (src[:, cols].astype(F32) + back).astype(BF)


def call(kernel, smem, dense, pieces, outs, scratch, flops=1024):
    vmem = pl.BlockSpec(memory_space=pltpu.VMEM)
    return pl.pallas_call(
        kernel,
        out_shape=[jax.ShapeDtypeStruct(shape, dtype) for shape, dtype in outs],
        in_specs=[pl.BlockSpec(memory_space=pltpu.SMEM)] * len(smem)
        + [vmem] * len(dense)
        + [pl.BlockSpec(memory_space=pl.ANY)] * len(pieces),
        out_specs=[vmem] * len(outs),
        scratch_shapes=scratch,
        compiler_params=pltpu.CompilerParams(vmem_limit_bytes=VMEM_LIMIT),
        cost_estimate=pl.CostEstimate(flops=flops, bytes_accessed=1024, transcendentals=0),
    )(*smem, *dense, *pieces)


def move(value, axes, target):
    sizes = [lax.axis_size(axis) for axis in axes]
    pairs = []
    for index in itertools.product(*[range(size) for size in sizes]):
        goal = target(*index)
        if goal is not None:
            flat = [0, 0]
            for size, a, b in zip(sizes, index, goal):
                flat = [flat[0] * size + a, flat[1] * size + b]
            pairs.append(tuple(flat))
    return lax.ppermute(value, axes, pairs)


def swap(value, axis, stride=1):
    count = lax.axis_size(axis)
    return lax.ppermute(value, axis, [(i, i ^ stride) for i in range(count)])


def rotate(value, axis, steps):
    count = lax.axis_size(axis)
    return lax.ppermute(value, axis, [(i, (i + steps) % count) for i in range(count)])


def over_fsdp(value):
    count = lax.axis_size("fsdp")
    return [value] + [rotate(value, "fsdp", -step) for step in range(1, count)]


def parity_half(value, parity, low, rows):
    return lax.dynamic_slice_in_dim(value, parity * (value.shape[0] // 2) + low, rows, 0)


def to_other_core(values, chosen):
    return [
        move(value, ("segment",), lambda s: (s ^ 1,) if s in chosen else None) for value in values
    ]


def small_exchange(wides, narrow, mesh_f, mesh_z):
    fsdp, dp = lax.axis_size("fsdp"), lax.axis_size("dp")
    rows, channels = wides[0].shape
    cut = channels // (fsdp * dp)
    wides = [wide.reshape(rows, fsdp, dp, cut).transpose(1, 2, 0, 3) for wide in wides]
    narrow = jnp.broadcast_to(narrow, (fsdp, dp) + narrow.shape)
    packed = jnp.concatenate([*wides, narrow], axis=3)
    parts = []
    for step in range(fsdp):
        part = lax.dynamic_index_in_dim(packed, (mesh_f - step) % fsdp, 0, keepdims=False)
        parts.append(rotate(part, "fsdp", -step) if step else part)
    parts = jnp.stack(parts, axis=1)
    found = []
    for step in range(dp):
        part = lax.dynamic_index_in_dim(parts, mesh_z ^ step, 0, keepdims=False)
        found.append(swap(part, "dp", step) if step else part)
    found = jnp.stack(found).reshape(-1, packed.shape[3])
    return found[:, : len(wides) * cut], found[:, len(wides) * cut :]


def on_device(inputs, cotangent, plan, weight, squeeze, excite):
    fsdp, dp = lax.axis_size("fsdp"), lax.axis_size("dp")
    sections = lax.axis_size("segment")
    section = lax.axis_index("segment")
    core, stage = section % 2, section // 2
    mesh_f, mesh_z = lax.axis_index("fsdp"), lax.axis_index("dp")
    micro, images_dev, pixels, channels = inputs.shape
    hidden = squeeze.shape[2]
    images = micro * images_dev // 2
    rows = up(images * pixels, 16)
    group = up(-(-channels // dp), 128)
    part = channels // fsdp
    tiles = [(low, min(group, channels - low)) for low in range(0, channels, group)]
    weight, squeeze, excite = weight[0], squeeze[0], excite[0]
    assert sections == 4 and dp & (dp - 1) == 0 and len(tiles) == dp
    fast = fsdp == 2 and dp % 2 == 0 and part % 32 == 0
    first_stage, last_stage = (0, 1), (2, 3)
    barrier = lax.optimization_barrier

    if fast:
        mine_at = mesh_f * part
        far_at = part - mine_at
        parity = mesh_z % 2
        half = part // 2
        near_at = far_at + parity * half
        cross_at = far_at + (1 - parity) * half
        near_s = [parity_half(side, parity, 0, half) for side in (squeeze, excite)]
        near_cut, inputs = barrier((jnp.concatenate(near_s, axis=0), inputs))
        s_at = [mine_at, near_at, cross_at]
        middle = half // 32 * 16
        cut_at = ((0, middle), (middle, half - middle))
        w_at = [mine_at, near_at, near_at + middle, cross_at, cross_at + middle]
    else:
        both = [lax.all_gather(side, "fsdp", axis=0, tiled=True) for side in (squeeze, excite)]
        s_own = [jnp.concatenate(both, axis=0)]
        s_other = [swap(s_own[0], "segment")]
        s_at = w_at = [jnp.int32(0)]
    n_w, n_s = len(w_at), len(s_at)

    def meta_for(at, where):
        fields = [core, (stage == where).astype(jnp.int32), mesh_f, *at]
        return jnp.stack([jnp.asarray(field, jnp.int32) for field in fields])

    slots = jnp.arange(micro, dtype=jnp.int32)
    back_order = jnp.sum(jnp.where(plan[None, :] == slots[:, None], slots[None, :], 0), axis=1)

    def flat(maps, order, send):
        maps = maps.transpose(0, 2, 1, 3).reshape(-1, channels)
        shape = ((rows, channels), BF)
        outs = [shape] + [((rows, part), BF)] * (2 * send)
        kernel = functools.partial(pick_kernel, (images, pixels, images_dev))
        smem = [meta_for([], 0), order.astype(jnp.int32)]
        return call(kernel, smem, [maps], [], outs, [])

    picked = flat(inputs, slots, fast)
    h_first = picked[0]

    saved_shapes = [
        ((rows, channels), F32),
        ((SUB, channels), F32),
        ((SUB, hidden), F32),
        ((SUB, channels), F32),
        ((SUB, hidden), F32),
    ]
    act_shape = pltpu.VMEM((rows, channels), BF)

    def weight_bufs(count, w_count):
        return [
            pltpu.VMEM((count, channels, channels), BF),
            pltpu.VMEM((2, channels, hidden), BF),
            pltpu.VMEM((2, channels, hidden), BF),
        ], [
            pltpu.SemaphoreType.DMA((count, len(tiles), w_count)),
            pltpu.SemaphoreType.DMA((2, 2, n_s)),
        ]

    def forward_pass(h_in, where, pieces):
        bufs, sems = weight_bufs(2, n_w)
        return call(
            functools.partial(forward_kernel, (n_w, n_s, images, pixels, tiles, fast)),
            [meta_for([*w_at, *s_at], where)],
            [h_in],
            pieces,
            [((rows, channels), BF)] * 2
            + saved_shapes * 2
            + [((rows, part), BF)] * (2 * fast),
            [*bufs, act_shape, *sems],
            PASS_FLOPS,
        )

    def backward_pass(d_out, saved, where, pieces, at, through):
        bufs, sems = weight_bufs(1 + through, len(at))
        outs = [((dp, rows, group), BF), ((SUB, hidden), F32), ((SUB, channels), F32)] * 2
        outs += [((rows, channels), BF)] * through
        return call(
            functools.partial(backward_kernel, (len(at), n_s, images, pixels, tiles, through)),
            [meta_for([*at, *s_at], where)],
            [d_out, *saved[0][:3], *saved[1][:3]],
            pieces,
            outs,
            [*bufs, act_shape, act_shape, *sems],
            PASS_FLOPS if through else 1024,
        )

    if fast:
        w_swapped = swap(weight, "segment")
        meta_s = meta_for(s_at, 0)
        mine, give = picked[1:]
        later_weight, give = barrier((weight, give))

        def near(index):
            cut = parity_half(later_weight, parity, *cut_at[index])
            return move(cut, ("segment", "fsdp"), lambda s, f: (s, 1 - f) if s > 1 else None)

        def cross(cut):
            return move(cut, ("segment", "dp"), lambda s, z: (s, z ^ 1) if s > 1 else None)

        near_w = [near(index) for index in range(len(cut_at))]

        def meet(give):
            return move(
                give, ("segment", "fsdp"), lambda s, f: (s, 1 - f) if s in first_stage else None
            )

        def share(block, mine, recv):
            shapes = [((rows, channels), F32), ((rows, channels), BF)]
            return call(
                functools.partial(share_kernel, block),
                [meta_s],
                [mine, recv],
                [weight, w_swapped],
                shapes,
                [
                    pltpu.VMEM((2 * rows, part), BF),
                    pltpu.VMEM((part, channels), BF),
                    pltpu.SemaphoreType.DMA((len(tiles),)),
                ],
            )

        def share_kernel(block, meta, mine_ref, recv_ref, own, other, *refs):
            partial_kernel((tiles,), block, meta, mine_ref, recv_ref, own, other, *refs)

        def finish(block, h_row, keep, recv):
            send = True
            outs = [((rows, channels), BF), *saved_shapes]
            outs += [((rows, part), BF)] * (2 * send)
            return call(
                functools.partial(gate_kernel, (n_s, images, pixels, tiles, send), block),
                [meta_s],
                [h_row, keep, recv],
                [*s_own, *s_other],
                outs,
                [
                    pltpu.VMEM((channels, hidden), BF),
                    pltpu.VMEM((channels, hidden), BF),
                    act_shape,
                    pltpu.SemaphoreType.DMA((2, n_s)),
                ],
            )

        recv_a, near_cut = barrier((meet(give), near_cut))
        near_s = swap(near_cut, "fsdp")
        own_s = jnp.concatenate([squeeze, excite], axis=0)
        other_s = jnp.concatenate([swap(side, "segment") for side in (squeeze, excite)], axis=0)
        mine, near_w[0], own_s, other_s = barrier((mine, near_w[0], own_s, other_s))
        keep, give = share(0, mine, recv_a)
        cross_w = [cross(near_w[0])]
        near_s, keep, cotangent = barrier((near_s, keep, cotangent))
        cross_s = swap(near_s, "dp")
        recv, cross_s = barrier((meet(give), cross_s))
        s_other = [other_s, swap(near_s, "segment"), swap(cross_s, "segment")]
        s_own = [own_s, near_s, cross_s]
        d_last = flat(cotangent, back_order, False)[0]
        keep, cross_w[0], near_w[1] = barrier((keep, cross_w[0], near_w[1]))
        result = finish(0, h_first, keep, recv)
        h_mid, saved_a = result[0], result[1:6]
        mid_mine, mid_give = result[6:]
        cross_w.append(cross(near_w[1]))
        recv_b = meet(mid_give)
        mid_mine, d_last = barrier((mid_mine, d_last))
        keep, give = share(1, mid_mine, recv_b)
        keep, cross_w[1] = barrier((keep, cross_w[1]))
        result = finish(1, h_mid, keep, meet(give))
        h_out, saved_b = result[0], result[1:6]
        out_mine, out_give = result[6:]
        h_in = move(h_out, ("segment",), lambda s: (s + 2,) if s < 2 else None)
        in_recv = move(
            out_give, ("segment", "fsdp"), lambda s, f: (s + 2, 1 - f) if s < 2 else None
        )
        late_weight, h_out = barrier((weight, h_out))
        far_late = [
            move(cut, ("segment", "fsdp"), lambda s, f: (s, 1 - f) if s == 1 else None)
            for cut in (late_weight[:half], late_weight[half:])
        ]
        far_early = near_w + cross_w
        late_at = [mine_at, far_at, far_at + half]
        early = [weight, *far_early, *s_own]
        early += [w_swapped, *to_other_core(far_early, last_stage), *s_other]
        first_units = [jnp.concatenate(pair, axis=0) for pair in ((mine, recv_a), (mid_mine, recv_b))]
    else:
        d_last = flat(cotangent, back_order, False)[0]
        whole = lax.all_gather(weight, "fsdp", axis=0, tiled=True)
        late_at = w_at
        early = late = [whole, *s_own, swap(whole, "segment"), *s_other]
        result = forward_pass(h_first, 0, early)
        h_mid, h_out, saved_a, saved_b = result[0], result[1], result[2:7], result[7:12]
        h_in = move(h_out, ("segment",), lambda s: (s + 2,) if s < 2 else None)
    first = (saved_a, saved_b)

    final = stage == 1

    def of_stage(ours, theirs):
        return jnp.where(final, ours, theirs)

    def fsdp_unit(value):
        found = []
        for step in range(fsdp):
            cut = lax.dynamic_slice_in_dim(value, ((mesh_f - step) % fsdp) * part, part, 1)
            found.append(rotate(cut, "fsdp", -step) if step else cut)
        return jnp.concatenate(found, axis=0)

    def dp_slots(unit):
        found = [unit] + [swap(unit, "dp", step) for step in range(1, dp if dp != 4 else 3)]
        if dp == 4:
            inner = lax.ppermute(unit, "dp", [(1, 2), (2, 1)])
            found.append(inner)
        return found

    def forwarded(slots):
        if dp != 4:
            return slots
        outer = lax.ppermute(slots[2], "dp", [(2, 3), (1, 0)])
        return slots[:3] + [jnp.where((mesh_z == 1) | (mesh_z == 2), slots[3], outer)]

    def swap_blocks(first, second):
        keep = jnp.where(core == 0, first, second)
        give = jnp.where(core == 0, second, first)
        return keep, swap(give, "segment")

    def both_cores(first, second):
        return jnp.concatenate(swap_blocks(first, second), axis=-2)

    if fast:
        in_mine = jnp.where(mesh_f == 0, h_in[:, :part], h_in[:, part:])
        unit = of_stage(jnp.concatenate([in_mine, in_recv], axis=0), first_units[0])
    else:
        unit = fsdp_unit(of_stage(h_in, h_first))
    h_in, unit = barrier((h_in, unit))
    slots_a = dp_slots(unit)
    result = forward_pass(h_in, 1, early)
    result, slots_a[:3], d_last = barrier((list(result), slots_a[:3], d_last))
    last = (result[2:7], result[7:12])
    if fast:
        mid_recv = move(
            result[13], ("segment", "fsdp"), lambda s, f: (s, 1 - f) if s > 1 else None
        )

    ended = list(backward_pass(d_last, last, 1, early, w_at, True))
    d_out = move(ended[6], ("segment",), lambda s: (s - 2,) if s > 1 else None)
    if fast:
        mid_recv, far_late, ended[1] = barrier((mid_recv, far_late, ended[1]))
        ours = jnp.concatenate([result[12], mid_recv], axis=0)
        unit = of_stage(ours, first_units[1])
        late_other = to_other_core(far_late, (1,))
        late = [weight, *far_late, *s_own, w_swapped, *late_other, *s_other]
    else:
        unit = fsdp_unit(of_stage(result[0], h_mid))
    slots_b = dp_slots(unit)
    slots_a = forwarded(slots_a)

    begun = backward_pass(d_out, first, 0, late, late_at, False)
    slots_b, begun = barrier((slots_b, begun))
    slots_b = forwarded(slots_b)
    h_all = []
    for slot_a, slot_b in zip(slots_a, slots_b):
        keep, other = swap_blocks(slot_a, slot_b)
        cuts = []
        for step in range(fsdp):
            cuts += [side[step * rows : (step + 1) * rows] for side in (keep, other)]
        h_all.append(jnp.concatenate(cuts, axis=0))
    found = [
        [of_stage(ended[3 * b + i], begun[3 * b + i]) for b in range(2)] for i in range(3)
    ]
    d_pre = both_cores(*found[0])
    small = []
    for b in range(2):
        pool, hid = [of_stage(last[b][i], first[b][i]) for i in (3, 4)]
        small.append(jnp.concatenate([pool, found[2][b], hid, found[1][b]], axis=1).astype(BF))
    small = both_cores(*small)
    pool, d_ex, hid_sq = jnp.split(small, (channels, 2 * channels), axis=1)

    total = None
    for step in range(dp):
        piece = lax.dynamic_index_in_dim(d_pre, mesh_z ^ step, 0, keepdims=False)
        if step:
            piece = swap(piece, "dp", step)
        piece = jnp.concatenate(over_fsdp(piece), axis=0)
        term = tn(h_all[step], piece)
        total = term if total is None else total + term
    total = total.astype(BF)
    own_rows = part // dp
    wide, hid_sq = small_exchange([pool, d_ex], hid_sq, mesh_f, mesh_z)
    grad_s = tn(wide[:, :own_rows], hid_sq[:, hidden:])
    grad_e = tn(wide[:, own_rows:], hid_sq[:, :hidden])
    gathered = jnp.zeros((dp, own_rows, group), BF)
    for step in range(dp):
        block = lax.dynamic_slice_in_dim(total, (mesh_z ^ step) * own_rows, own_rows, 0)
        if step:
            block = swap(block, "dp", step)
        gathered = lax.dynamic_update_index_in_dim(gathered, block, mesh_z ^ step, 0)
    grad_w = jnp.concatenate([gathered[i, :, :w] for i, (_, w) in enumerate(tiles)], axis=1)
    return (grad_w.astype(F32)[None], grad_s[None], grad_e[None])


def solution(mesh):
    placed = (
        P(None, ("fsdp", "dp"), None, None),
        P(None, ("fsdp", "dp"), None, None),
        P(),
        P("segment", "fsdp", None),
        P("segment", "fsdp", None),
        P("segment", "fsdp", None),
    )
    return jax.shard_map(
        on_device,
        mesh=mesh,
        in_specs=placed,
        out_specs=(
            P("segment", ("fsdp", "dp"), None),
            P("segment", ("fsdp", "dp"), None),
            P("segment", ("fsdp", "dp"), None),
        ),
        check_vma=False,
    )
```
